256 devices in a mesh: ctx: 16 (over x, y), dp: 16 (over z, core).
Axes of the slice: x: 4, y: 4, z: 8, core: 2. Of those that a mesh axis runs over, the one named last changes fastest.
Arguments:
- inputs: bfloat16 [32, 2048, 1024], P('dp', 'ctx'), may hold values from -6 to 6
- gate_in: bfloat16 [32, 2048, 1024], P('dp', 'ctx'), may hold values from -6 to 6
- cotangent: bfloat16 [32, 2048, 1024], P('dp', 'ctx'), may hold values from -6 to 6
- recon_mask: int32 [32, 2048], P('dp', 'ctx'), may hold values 0 or 1
- segment_starts: int32 [32, 3], P('dp'), may hold values from 1 to 2047
- weights: bfloat16 [1024, 2048], replicated, may hold values from -0.1875 to 0.1875
- gate_bias: float32 [2048], replicated, may hold values from -4 to 4
- decay_rate: float32 [1024], replicated, may hold values from 9.765625e-07 to 0.01
Outputs:
- input_grad: bfloat16 [32, 2048, 1024], P('dp', 'ctx')
- gate_grad: bfloat16 [32, 2048, 1024], P('dp', 'ctx')
- weight_grads: float32 [1024, 2048], P('ctx', 'dp')
The draws below stay inside these ranges and needn't reach their ends.
Inputs may be any that keep to these rules, and one draw needn't show every extreme that they name: `segment_starts`: each entry is a position of its row at which a new packed sequence begins; entries may repeat and come in any order.
All inputs are finite; a program needn't handle non-finite values. No bound on the sum of `recon_mask` on one device may be relied on, other than what follows from the above.
Results may differ from the reference program's by a relative error of at most 0.0044.
Values sent between devices are 32-bit elements; how exact they have to be, the bound alone decides.
No kernel may reach another device: no remote copies, remote signals or barrier semaphores. Data moves between devices by JAX's collectives and lax.ppermute only.
A program may use at most 128 MiB of HBM per device.

```python
import math
import jax
import jax.numpy as jnp
from jax import lax

D = 1024
SEGS = 3
ROWS = 32
SEQLEN = 2048


def place_ends(array, stream_key, smallest, top_value):
    spot = [jax.random.randint(jax.random.fold_in(stream_key, axis), (), 0, length) for axis, length in enumerate(array.shape)]
    main_axis = array.shape.index(max(array.shape))
    neighbour = spot[:main_axis] + [(spot[main_axis] + 1) % array.shape[main_axis]] + spot[main_axis + 1:]
    return array.at[tuple(spot)].set(smallest).at[tuple(neighbour)].set(top_value)


def spiked(array, stream_key, source, target, blocks, factor):
    def block_of(dim):
        return (jnp.arange(array.shape[dim]) // (array.shape[dim] // blocks)).reshape((-1,) + (1,) * (array.ndim - 1 - dim))

    first = jax.random.permutation(stream_key, blocks)[block_of(target)]
    second = (block_of(target) + blocks // 2) % blocks
    return jnp.where((block_of(source) == first) | (block_of(source) == second), factor * array, array)


def block_scale(stream_key, dims, pieces, least, largest):
    factor_of = 1.0
    for dim, shards_of in pieces:
        steps = jax.random.uniform(jax.random.fold_in(jax.random.fold_in(stream_key, 6), dim), (shards_of,), jnp.float32, least / len(pieces), largest / len(pieces))
        factor_of = factor_of * jnp.repeat(jnp.exp(steps), dims[dim] // shards_of).reshape((-1,) + (1,) * (len(dims) - 1 - dim))
    return factor_of


def normal_values(rng, shape, scale, bound, shards=(), kind=jnp.bfloat16):
    entries = jax.random.normal(rng, shape, jnp.float32) * scale
    if len(shards) > 0:
        entries = block_scale(rng, shape, shards, -0.22, 0.18) * entries
    return jnp.clip(entries, min=-bound, max=bound).astype(kind)


def noise_with(key, extent, width, most, cuts, heavy, kind=jnp.bfloat16):
    entries = width * jax.random.normal(key, extent, jnp.float32)
    if cuts:
        entries = entries * block_scale(key, extent, cuts, -0.22, 0.18)
    return jnp.clip(spiked(entries, jax.random.fold_in(key, 3), *heavy), -most, most).astype(kind)


def setup_inputs(seed: int = 0) -> dict:
    splits = jax.random.split(jax.random.key(seed), 9)
    inputs = noise_with(splits[0], (ROWS, SEQLEN, D), 1.0, 6.0, ((0, 16), (1, 16)), (1, 2, 16, 2.0))
    gate_in = normal_values(splits[1], (ROWS, SEQLEN, D), 1.0, 6.0, ((0, 16), (1, 16)))
    cotangent = noise_with(splits[2], (ROWS, SEQLEN, D), 1.0, 6.0, ((0, 16), (1, 16)), (0, 2, 16, 2.0))
    recon_mask = place_ends((jax.random.randint(splits[3], (ROWS, SEQLEN), 0, 4) < 3).astype(jnp.int32), jax.random.fold_in(splits[3], 1), 0, 1)
    segment_starts = place_ends(jax.random.randint(splits[4], (ROWS, SEGS), 1, SEQLEN), jax.random.fold_in(splits[4], 1), 1, SEQLEN - 1).astype(jnp.int32)
    weights = normal_values(splits[5], (D, 2 * D), D ** -0.5, 0.1875)
    gate_bias = normal_values(splits[6], (2 * D,), 1.0, 4.0, (), jnp.float32)
    decay_rate = jnp.clip(jnp.exp(jax.random.uniform(splits[7], (D,), jnp.float32, math.log(9.765625463842298e-07), math.log(0.01))), 9.765625463842298e-07, 0.01)
    return {"inputs": inputs, "gate_in": gate_in, "cotangent": cotangent, "recon_mask": recon_mask, "segment_starts": segment_starts, "weights": weights, "gate_bias": gate_bias, "decay_rate": decay_rate}


def combine(earlier, latter):
    return (earlier[0] * latter[0], latter[0] * earlier[1] + latter[1])

def row_backward(x_row, gate_row, cot_row, mask_row, starts_row, weights, gate_bias, decay_rate):
    model_width = x_row.shape[1]
    preact = jnp.dot(x_row, weights, preferred_element_type=jnp.float32) + gate_bias
    gate_decay = jax.nn.sigmoid(preact[:, :model_width])
    gate_input = jax.nn.sigmoid(preact[:, model_width:])
    position = jnp.arange(x_row.shape[0], dtype=jnp.int32)
    start_hit = jnp.any(position[:, None] == starts_row[None, :], axis=1) | (position == 0)
    reset_flag = start_hit.astype(jnp.float32)[:, None]
    carry_keep = 1.0 - reset_flag
    decay_arg = 8.0 * decay_rate * gate_decay
    decay_step = jnp.exp(-decay_arg)
    step_decay = carry_keep * decay_step
    norm_square = -jnp.expm1(-2.0 * decay_arg)
    input_norm = reset_flag + carry_keep * jnp.sqrt(norm_square)
    inputs_wide = x_row.astype(jnp.float32)
    drive_term = input_norm * gate_input * inputs_wide
    hidden = lax.associative_scan(combine, (step_decay, drive_term), axis=0)[1]
    hidden_prev = jnp.concatenate([jnp.zeros_like(hidden[:1]), hidden[:-1]], axis=0)
    grad_out = mask_row.astype(jnp.float32)[:, None] * cot_row.astype(jnp.float32)
    gelu_value, gelu_back = jax.vjp(jax.nn.gelu, gate_row.astype(jnp.float32))
    grad_hidden = grad_out * gelu_value
    gate_grad = gelu_back(grad_out * hidden)[0].astype(jnp.bfloat16)
    carried = lax.associative_scan(combine, (step_decay, step_decay * grad_hidden), axis=0, reverse=True)[1]
    adjoint = grad_hidden + jnp.concatenate([carried[1:], jnp.zeros_like(carried[:1])], axis=0)
    ratio_term = decay_arg / norm_square
    grad_decay_gate = (1.0 - gate_decay) * decay_arg * (carry_keep * decay_step * decay_step * input_norm * ratio_term * adjoint * gate_input * inputs_wide - step_decay * adjoint * hidden_prev)
    grad_input_gate = adjoint * input_norm * inputs_wide * gate_input * (1.0 - gate_input)
    grad_preact = jnp.concatenate([grad_decay_gate, grad_input_gate], axis=-1).astype(jnp.bfloat16)
    back_term = jnp.dot(grad_preact, weights.T, preferred_element_type=jnp.float32)
    input_grad = (adjoint * input_norm * gate_input + back_term).astype(jnp.bfloat16)
    return (input_grad, gate_grad, grad_preact)

def reference(inputs, gate_in, cotangent, recon_mask, segment_starts, weights, gate_bias, decay_rate):

    def one_row(total, row_items):
        x_row, gate_row, cot_row, mask_row, starts_row = row_items
        input_grad, gate_grad, grad_preact = row_backward(x_row, gate_row, cot_row, mask_row, starts_row, weights, gate_bias, decay_rate)
        total = total + jnp.dot(x_row.T, grad_preact, preferred_element_type=jnp.float32)
        return (total, (input_grad, gate_grad))
    start_total = jnp.zeros((D, 2 * D), jnp.float32)
    total, outputs = lax.scan(one_row, start_total, (inputs, gate_in, cotangent, recon_mask, segment_starts))
    scale_factor = 1.0 / math.sqrt(ROWS * SEQLEN)
    return (outputs[0], outputs[1], total * scale_factor)
```

```python
import math

import jax
import jax.numpy as jnp
from jax import lax
from jax.experimental import pallas as pl
from jax.experimental.pallas import tpu as pltpu
from jax.sharding import PartitionSpec as P

GROUPS = 8
LANES = 128
BLOCK = 256
F32 = jnp.float32
BF16 = jnp.bfloat16
ROOT = math.sqrt(2.0 / math.pi)
CUBIC = 0.044715


def dot(a, b, dims=((1,), (0,))):
    return lax.dot_general(a, b, (dims, ((), ())), preferred_element_type=F32)


def order(tokens, steps, transpose=False):
    inner = steps // GROUPS
    rho = lax.broadcasted_iota(jnp.int32, (tokens, tokens), 1 if transpose else 0)
    at = lax.broadcasted_iota(jnp.int32, (tokens, tokens), 0 if transpose else 1)
    place = rho % steps
    source = (rho - place) + (place % GROUPS) * inner + place // GROUPS
    return at == source


def wide(value, width):
    return jnp.concatenate([value] * (width // value.shape[1]), axis=1)


def logistic(value):
    return 0.5 * jnp.tanh(0.5 * value) + 0.5


def gates_kernel(
    starts, x, gin, cot, mask, w_decay, w_input, b_decay, b_input, rate,
    summary, grouped, a_out, c_out, f_out, ru_out, q_out, gh_out, gg_out, xp_out,
    move, move_masked, xb, p1, p2, gins, gos,
):
    tokens, steps = x.shape[0], mask.shape[1]
    rows, inner = tokens // steps, steps // GROUPS
    width = gin.shape[1]
    block = pl.program_id(0)
    base = lax.axis_index("ctx") * steps

    @pl.when(block == 0)
    def _():
        hit = order(tokens, steps)
        masks = mask[...].astype(F32)
        mask_row = jnp.concatenate([masks[r : r + 1] for r in range(rows)], axis=1)
        move[...] = jnp.where(hit, 1.0, 0.0).astype(BF16)
        move_masked[...] = jnp.where(hit, jnp.broadcast_to(mask_row, hit.shape), 0.0).astype(BF16)
        xp_out[...] = dot(move[...], x[...])
        xb[...] = xp_out[...].astype(BF16)

    p1[...] = dot(xb[...], w_decay[...]) + b_decay[...]
    p2[...] = dot(xb[...], w_input[...]) + b_input[...]
    gins[...] = dot(move[...], gin[...])
    gos[...] = dot(move_masked[...], cot[...])
    rate8 = jnp.broadcast_to(8.0 * rate[...], (GROUPS, width))
    spot = lax.broadcasted_iota(jnp.int32, (GROUPS, LANES), 0) * inner + base
    lanes = pl.ds(pl.multiple_of(block * width, width), width)

    def ahead(k, carry):
        new = []
        for r in range(rows):
            h, prod = carry[2 * r], carry[2 * r + 1]
            at = pl.ds(pl.multiple_of(r * steps + k * GROUPS, GROUPS), GROUPS)
            here = spot + k
            reset = here == 0
            for s in range(starts.shape[1]):
                reset = reset | (here == starts[r, s])
            keep = wide(jnp.where(reset, 0.0, 1.0), width)
            gate_decay = logistic(p1[at, :])
            gate_input = logistic(p2[at, :])
            xt = xp_out[at, lanes]
            arg = rate8 * gate_decay
            y = 2.0 * arg
            step = jnp.exp(-arg)
            square = y * (
                1.0 - y * (1 / 2 - y * (1 / 6 - y * (1 / 24 - y * (1 / 120 - y * (1 / 720)))))
            )
            a = keep * step
            c = ((1.0 - keep) + keep * jnp.sqrt(square)) * gate_input
            u = c * xt
            ratio = 0.5 + y * (0.25 + y * (1 / 24 - (y * y) * (1 / 1440)))
            a_out[at, :] = a
            c_out[at, :] = c
            f_out[at, :] = (1.0 - gate_decay) * arg * a
            ru_out[at, :] = a * ratio * u
            q_out[at, :] = u * (1.0 - gate_input)
            new += [a * h + u, a * prod]
            g, go = gins[at, :], gos[at, :]
            gsq = g * g
            th = jnp.tanh(ROOT * g * (1.0 + CUBIC * gsq))
            half = 0.5 * (1.0 + th)
            gh_out[at, :] = go * (g * half)
            gg_out[at, :] = go * (
                half + 0.5 * g * (1.0 - th * th) * (ROOT * (1.0 + (3.0 * CUBIC) * gsq))
            )
        return tuple(new)

    zero = jnp.zeros((GROUPS, width), F32)
    one = jnp.ones((GROUPS, width), F32)
    forward = lax.fori_loop(0, inner, ahead, (zero, one) * rows, unroll=2)

    def back(i, carry):
        k = inner - 1 - i
        new = []
        for r in range(rows):
            at = pl.ds(pl.multiple_of(r * steps + k * GROUPS, GROUPS), GROUPS)
            new.append(a_out[at, :] * (gh_out[at, :] + carry[r]))
        return tuple(new)

    backward = lax.fori_loop(0, inner, back, (zero,) * rows, unroll=4)

    for r in range(rows):
        hs, ps, bs = forward[2 * r], forward[2 * r + 1], backward[r]
        grouped[pl.ds((0 * rows + r) * GROUPS, GROUPS), :] = ps
        grouped[pl.ds((1 * rows + r) * GROUPS, GROUPS), :] = hs
        grouped[pl.ds((2 * rows + r) * GROUPS, GROUPS), :] = bs
        qs = ps
        for d in (1, 2, 4):
            hs = ps * pltpu.roll(hs, d, 0) + hs
            ps = ps * pltpu.roll(ps, d, 0)
            bs = qs * pltpu.roll(bs, GROUPS - d, 0) + bs
            qs = qs * pltpu.roll(qs, GROUPS - d, 0)
        summary[0 * rows + r : 0 * rows + r + 1, :] = ps[GROUPS - 1 :]
        summary[1 * rows + r : 1 * rows + r + 1, :] = hs[GROUPS - 1 :]
        summary[2 * rows + r : 2 * rows + r + 1, :] = bs[:1]


def grads_kernel(
    slabs, grouped, a_in, c_in, f_in, ru_in, q_in, gh_in, gg_in, xp,
    gate_grad, grads, sent, direct,
    prev, ggs, gds, gis,
):
    count = slabs.shape[0]
    rows = slabs.shape[1] // 3
    tokens, width = a_in.shape
    steps = tokens // rows
    inner = steps // GROUPS
    me = lax.axis_index("ctx")
    sub = lax.broadcasted_iota(jnp.int32, (GROUPS, width), 0)

    def spread(i, row):
        return jnp.broadcast_to(slabs[i, row : row + 1, :], (GROUPS, width))

    enter, enter_back = [], []
    for r in range(rows):
        h = jnp.zeros((GROUPS, width), F32)
        for i in range(count - 1):
            h = jnp.where(i < me, spread(i, r) * h + spread(i, rows + r), h)
        b = jnp.zeros((GROUPS, width), F32)
        for i in range(count - 1, 0, -1):
            b = jnp.where(i > me, spread(i, r) * b + spread(i, 2 * rows + r), b)
        ps = grouped[pl.ds((0 * rows + r) * GROUPS, GROUPS), :]
        hs = grouped[pl.ds((1 * rows + r) * GROUPS, GROUPS), :]
        bs = grouped[pl.ds((2 * rows + r) * GROUPS, GROUPS), :]
        hs = jnp.where(sub == 0, ps * h + hs, hs)
        bs = jnp.where(sub == GROUPS - 1, ps * b + bs, bs)
        qs = ps
        for d in (1, 2, 4):
            hs = jnp.where(sub >= d, ps * pltpu.roll(hs, d, 0) + hs, hs)
            ps = jnp.where(sub >= d, ps * pltpu.roll(ps, d, 0), ps)
            bs = jnp.where(sub < GROUPS - d, qs * pltpu.roll(bs, GROUPS - d, 0) + bs, bs)
            qs = jnp.where(sub < GROUPS - d, qs * pltpu.roll(qs, GROUPS - d, 0), qs)
        enter.append(jnp.where(sub == 0, h, pltpu.roll(hs, 1, 0)))
        enter_back.append(jnp.where(sub == GROUPS - 1, b, pltpu.roll(bs, GROUPS - 1, 0)))

    def ahead(k, carry):
        new = []
        for r in range(rows):
            at = pl.ds(pl.multiple_of(r * steps + k * GROUPS, GROUPS), GROUPS)
            prev[at, :] = carry[r]
            h = a_in[at, :] * carry[r] + c_in[at, :] * xp[at, :]
            ggs[at, :] = gg_in[at, :] * h
            new.append(h)
        return tuple(new)

    lax.fori_loop(0, inner, ahead, tuple(enter), unroll=4)

    def back(i, carry):
        k = inner - 1 - i
        new = []
        for r in range(rows):
            at = pl.ds(pl.multiple_of(r * steps + k * GROUPS, GROUPS), GROUPS)
            adjoint = gh_in[at, :] + carry[r]
            new.append(a_in[at, :] * adjoint)
            gds[at, :] = adjoint * f_in[at, :] * (ru_in[at, :] - prev[at, :])
            gis[at, :] = adjoint * q_in[at, :]
            direct[at, :] = adjoint * c_in[at, :]
        return tuple(new)

    lax.fori_loop(0, inner, back, tuple(enter_back), unroll=4)
    unmove = jnp.where(order(tokens, steps, True), 1.0, 0.0).astype(BF16)
    gate_grad[...] = dot(unmove, ggs[...].astype(BF16)).astype(BF16)
    other = lax.axis_index("dp") % 2 == 0
    for half, value in enumerate((gds, gis)):
        grads[half] = value[...].astype(BF16)
        sent[half] = jnp.where(other, value[:, LANES:], value[:, :LANES])


def weights_kernel(x_own, x_other, grads, received, out, held):
    tokens = x_own.shape[0]

    @pl.when(pl.program_id(0) == 0)
    def _():
        core = lax.axis_index("dp") % 2
        parts = grads.shape[2] // (2 * LANES)
        for half in range(2):
            for z in range(parts):
                to = pl.ds((half * parts + z) * LANES, LANES)
                came = pl.ds(z * LANES, LANES)
                own = jnp.where(
                    core == 0,
                    grads[half, :, pl.ds(2 * z * LANES, LANES)].astype(F32),
                    grads[half, :, pl.ds((2 * z + 1) * LANES, LANES)].astype(F32),
                )
                held[pl.ds(0, tokens), to] = own.astype(BF16)
                held[pl.ds(tokens, tokens), to] = received[half, :, came].astype(BF16)

    both = jnp.concatenate([x_own[...].astype(BF16), x_other[...].astype(BF16)], axis=0)
    out[...] = dot(both, held[...], ((0,), (0,)))


def inputs_kernel(steps, grads, direct, weights, out):
    width = grads.shape[2]
    tokens = direct.shape[0]
    total = direct[...]
    for half in range(2):
        total = total + dot(
            grads[half], weights[:, half * width : (half + 1) * width], ((1,), (1,))
        )
    unmove = jnp.where(order(tokens, steps, True), 1.0, 0.0).astype(BF16)
    out[...] = dot(unmove, total.astype(BF16)).astype(BF16)


def sum_kernel(at, parts, out):
    total = parts[0]
    for i in range(1, parts.shape[0]):
        total = total + parts[i]
    out[0] = total


def params(mib):
    return pltpu.CompilerParams(vmem_limit_bytes=mib << 20)


def full(shape):
    return pl.BlockSpec(shape, lambda j: (0,) * len(shape))


def columns(rows, width=BLOCK, first=0):
    return pl.BlockSpec((rows, width), lambda j: (0, j + first))


def shaped(shape, dtype=F32):
    return jax.ShapeDtypeStruct(shape, dtype)


def per_device(
    inputs, gate_in, cotangent, recon_mask, segment_starts, weights, gate_bias, decay_rate
):
    rows, steps, model = inputs.shape
    tokens = rows * steps
    peers, pairs = lax.axis_size("ctx"), lax.axis_size("dp")
    chips = pairs // 2
    blocks = model // BLOCK
    flat = lambda value: value.reshape(tokens, model)
    bias = gate_bias.reshape(1, 2 * model)
    big = shaped((tokens, model))
    tile = columns(tokens)
    outs = pl.pallas_call(
        gates_kernel,
        grid=(blocks,),
        in_specs=[
            pl.BlockSpec(memory_space=pltpu.SMEM),
            full((tokens, model)),
            tile,
            tile,
            full((rows, steps)),
            columns(model),
            columns(model, first=blocks),
            columns(1),
            columns(1, first=blocks),
            columns(1),
        ],
        out_specs=[columns(3 * rows), columns(3 * rows * GROUPS)] + [tile] * 7 + [full((tokens, model))],
        out_shape=[shaped((3 * rows, model)), shaped((3 * rows * GROUPS, model))] + [big] * 8,
        scratch_shapes=[
            pltpu.VMEM((tokens, tokens), BF16),
            pltpu.VMEM((tokens, tokens), BF16),
            pltpu.VMEM((tokens, model), BF16),
        ]
        + [pltpu.VMEM((tokens, BLOCK), F32)] * 4,
        compiler_params=params(32),
        name="gates",
    )(
        segment_starts, flat(inputs), flat(gate_in), flat(cotangent), recon_mask,
        weights, weights, bias, bias, decay_rate.reshape(1, model),
    )
    summary, grouped, *middle, xp = outs
    swap = [(i, i ^ 1) for i in range(pairs)]
    x_other = lax.ppermute(xp, "dp", swap)
    slabs = lax.all_to_all(
        jnp.broadcast_to(summary, (peers,) + summary.shape), "ctx", 0, 0, tiled=True
    )
    pair_tile = pl.BlockSpec((2, tokens, BLOCK), lambda j: (0, 0, j))
    gate_grad, grads, sent, direct = pl.pallas_call(
        grads_kernel,
        grid=(blocks,),
        in_specs=[
            pl.BlockSpec((peers, 3 * rows, BLOCK), lambda j: (0, 0, j)),
            columns(3 * rows * GROUPS),
        ]
        + [tile] * 8,
        out_specs=[
            tile,
            pair_tile,
            pl.BlockSpec((2, tokens, LANES), lambda j: (0, 0, j)),
            tile,
        ],
        out_shape=[
            shaped((tokens, model), BF16),
            shaped((2, tokens, model), BF16),
            shaped((2, tokens, model // 2)),
            big,
        ],
        scratch_shapes=[pltpu.VMEM((tokens, BLOCK), F32)] * 4,
        compiler_params=params(32),
        name="grads",
    )(slabs, grouped, *middle, xp)
    received = lax.ppermute(sent, "dp", swap)
    partial = pl.pallas_call(
        weights_kernel,
        grid=(blocks,),
        in_specs=[tile, tile, full((2, tokens, model)), full((2, tokens, model // 2))],
        out_specs=pl.BlockSpec((BLOCK, model), lambda j: (j, 0)),
        out_shape=shaped((model, model)),
        scratch_shapes=[pltpu.VMEM((2 * tokens, model), BF16)],
        compiler_params=params(24),
        name="weights",
    )(xp, x_other, grads, received)
    part = model // peers
    slices = lax.all_to_all(partial.reshape(peers, part, model), "ctx", 0, 0, tiled=True)
    chip = lax.axis_index("dp") // 2
    by_chip = pl.pallas_call(
        sum_kernel,
        grid_spec=pltpu.PrefetchScalarGridSpec(
            num_scalar_prefetch=1,
            grid=(chips,),
            in_specs=[
                pl.BlockSpec((peers, part, LANES), lambda j, at: (0, 0, lax.rem(j + at[0], chips)))
            ],
            out_specs=pl.BlockSpec((1, part, LANES), lambda j, at: (j, 0, 0)),
        ),
        out_shape=shaped((chips, part, LANES)),
        compiler_params=params(16),
        name="slab_sum",
    )(chip.reshape(1), slices)
    total = by_chip[0]
    for d in range(1, chips):
        hop = [(i, ((i // 2 + d) % chips) * 2 + i % 2) for i in range(pairs)]
        total = total + lax.ppermute(by_chip[d], "dp", hop)
    scale = 1.0 / math.sqrt(rows * pairs * steps * peers)
    input_grad = pl.pallas_call(
        lambda *refs: inputs_kernel(steps, *refs),
        grid=(blocks,),
        in_specs=[
            full((2, tokens, model)),
            tile,
            pl.BlockSpec((BLOCK, 2 * model), lambda j: (j, 0)),
        ],
        out_specs=tile,
        out_shape=shaped((tokens, model), BF16),
        compiler_params=params(24),
        name="inputs",
    )(grads, direct, weights)
    return (
        input_grad.reshape(inputs.shape),
        gate_grad.reshape(inputs.shape),
        total * scale,
    )


def solution(mesh):
    return jax.shard_map(
        per_device,
        mesh=mesh,
        in_specs=(
            P("dp", "ctx", None),
            P("dp", "ctx", None),
            P("dp", "ctx", None),
            P("dp", "ctx"),
            P("dp", None),
            P(),
            P(),
            P(),
        ),
        out_specs=(P("dp", "ctx", None), P("dp", "ctx", None), P("ctx", "dp")),
        check_vma=False,
    )
```

```python
import math

import jax
import jax.numpy as jnp
from jax import lax
from jax.experimental import pallas as pl
from jax.experimental.pallas import tpu as pltpu
from jax.sharding import PartitionSpec as P

GROUPS = 8
LANES = 128
BLOCK = 256
F32 = jnp.float32
BF16 = jnp.bfloat16
ROOT = math.sqrt(2.0 / math.pi)
CUBIC = 0.044715
SIDE = 4
PIECES = (8, 10, 6, 12, 4, 14, 0)


def dot(a, b, dims=((1,), (0,))):
    return lax.dot_general(a, b, (dims, ((), ())), preferred_element_type=F32)


def order(tokens, steps, transpose=False):
    inner = steps // GROUPS
    rho = lax.broadcasted_iota(jnp.int32, (tokens, tokens), 1 if transpose else 0)
    at = lax.broadcasted_iota(jnp.int32, (tokens, tokens), 0 if transpose else 1)
    place = rho % steps
    source = (rho - place) + (place % GROUPS) * inner + place // GROUPS
    return at == source


def wide(value, width):
    return jnp.concatenate([value] * (width // value.shape[1]), axis=1)


def logistic(value):
    return 0.5 * jnp.tanh(0.5 * value) + 0.5


def gates_kernel(
    starts, x, gin, cot, mask, w_decay, w_input, b_decay, b_input, rate,
    summary, grouped, a_out, c_out, f_out, ru_out, q_out, gh_out, gg_out, xp_out,
    move, move_masked, xb, p1, p2, gins, gos,
):
    tokens, steps = x.shape[0], mask.shape[1]
    rows, inner = tokens // steps, steps // GROUPS
    width = gin.shape[1]
    block = pl.program_id(0)
    base = lax.axis_index("ctx") * steps

    @pl.when(block == 0)
    def _():
        hit = order(tokens, steps)
        masks = mask[...].astype(F32)
        mask_row = jnp.concatenate([masks[r : r + 1] for r in range(rows)], axis=1)
        move[...] = jnp.where(hit, 1.0, 0.0).astype(BF16)
        move_masked[...] = jnp.where(hit, jnp.broadcast_to(mask_row, hit.shape), 0.0).astype(BF16)
        xp_out[...] = dot(move[...], x[...])
        xb[...] = xp_out[...].astype(BF16)

    p1[...] = dot(xb[...], w_decay[...]) + b_decay[...]
    p2[...] = dot(xb[...], w_input[...]) + b_input[...]
    gins[...] = dot(move[...], gin[...])
    gos[...] = dot(move_masked[...], cot[...])
    rate8 = jnp.broadcast_to(8.0 * rate[...], (GROUPS, width))
    spot = lax.broadcasted_iota(jnp.int32, (GROUPS, LANES), 0) * inner + base
    lanes = pl.ds(pl.multiple_of(block * width, width), width)

    def ahead(k, carry):
        new = []
        for r in range(rows):
            h, prod = carry[2 * r], carry[2 * r + 1]
            at = pl.ds(pl.multiple_of(r * steps + k * GROUPS, GROUPS), GROUPS)
            here = spot + k
            reset = here == 0
            for s in range(starts.shape[1]):
                reset = reset | (here == starts[r, s])
            keep = wide(jnp.where(reset, 0.0, 1.0), width)
            gate_decay = logistic(p1[at, :])
            gate_input = logistic(p2[at, :])
            xt = xp_out[at, lanes]
            arg = rate8 * gate_decay
            y = 2.0 * arg
            step = jnp.exp(-arg)
            square = y * (
                1.0 - y * (1 / 2 - y * (1 / 6 - y * (1 / 24 - y * (1 / 120 - y * (1 / 720)))))
            )
            a = keep * step
            c = ((1.0 - keep) + keep * jnp.sqrt(square)) * gate_input
            u = c * xt
            ratio = 0.5 + y * (0.25 + y * (1 / 24 - (y * y) * (1 / 1440)))
            a_out[at, :] = a
            c_out[at, :] = c
            f_out[at, :] = (1.0 - gate_decay) * arg * a
            ru_out[at, :] = a * ratio * u
            q_out[at, :] = u * (1.0 - gate_input)
            new += [a * h + u, a * prod]
            g, go = gins[at, :], gos[at, :]
            gsq = g * g
            th = jnp.tanh(ROOT * g * (1.0 + CUBIC * gsq))
            half = 0.5 * (1.0 + th)
            gh_out[at, :] = go * (g * half)
            gg_out[at, :] = go * (
                half + 0.5 * g * (1.0 - th * th) * (ROOT * (1.0 + (3.0 * CUBIC) * gsq))
            )
        return tuple(new)

    zero = jnp.zeros((GROUPS, width), F32)
    one = jnp.ones((GROUPS, width), F32)
    forward = lax.fori_loop(0, inner, ahead, (zero, one) * rows, unroll=2)

    def back(i, carry):
        k = inner - 1 - i
        new = []
        for r in range(rows):
            at = pl.ds(pl.multiple_of(r * steps + k * GROUPS, GROUPS), GROUPS)
            new.append(a_out[at, :] * (gh_out[at, :] + carry[r]))
        return tuple(new)

    backward = lax.fori_loop(0, inner, back, (zero,) * rows, unroll=4)

    for r in range(rows):
        hs, ps, bs = forward[2 * r], forward[2 * r + 1], backward[r]
        grouped[pl.ds((0 * rows + r) * GROUPS, GROUPS), :] = ps
        grouped[pl.ds((1 * rows + r) * GROUPS, GROUPS), :] = hs
        grouped[pl.ds((2 * rows + r) * GROUPS, GROUPS), :] = bs
        qs = ps
        for d in (1, 2, 4):
            hs = ps * pltpu.roll(hs, d, 0) + hs
            ps = ps * pltpu.roll(ps, d, 0)
            bs = qs * pltpu.roll(bs, GROUPS - d, 0) + bs
            qs = qs * pltpu.roll(qs, GROUPS - d, 0)
        for i, value in enumerate((ps[GROUPS - 1 :], hs[GROUPS - 1 :], bs[:1])):
            at = pl.ds(i * rows + r, 1)
            summary[:, at, :] = jnp.broadcast_to(value[None], (summary.shape[0], 1, width))


def grads_kernel(
    slabs, grouped, a_in, c_in, f_in, ru_in, q_in, gh_in, gg_in, xp,
    gate_grad, grads, sent, direct,
    prev, ggs, gds, gis,
):
    count = slabs.shape[0]
    rows = slabs.shape[1] // 3
    tokens, width = a_in.shape
    steps = tokens // rows
    inner = steps // GROUPS
    me = lax.axis_index("ctx")
    sub = lax.broadcasted_iota(jnp.int32, (GROUPS, width), 0)

    def spread(i, row):
        return jnp.broadcast_to(slabs[i, row : row + 1, :], (GROUPS, width))

    enter, enter_back = [], []
    for r in range(rows):
        h = jnp.zeros((GROUPS, width), F32)
        for i in range(count - 1):
            h = jnp.where(i < me, spread(i, r) * h + spread(i, rows + r), h)
        b = jnp.zeros((GROUPS, width), F32)
        for i in range(count - 1, 0, -1):
            b = jnp.where(i > me, spread(i, r) * b + spread(i, 2 * rows + r), b)
        ps = grouped[pl.ds((0 * rows + r) * GROUPS, GROUPS), :]
        hs = grouped[pl.ds((1 * rows + r) * GROUPS, GROUPS), :]
        bs = grouped[pl.ds((2 * rows + r) * GROUPS, GROUPS), :]
        hs = jnp.where(sub == 0, ps * h + hs, hs)
        bs = jnp.where(sub == GROUPS - 1, ps * b + bs, bs)
        qs = ps
        for d in (1, 2, 4):
            hs = jnp.where(sub >= d, ps * pltpu.roll(hs, d, 0) + hs, hs)
            ps = jnp.where(sub >= d, ps * pltpu.roll(ps, d, 0), ps)
            bs = jnp.where(sub < GROUPS - d, qs * pltpu.roll(bs, GROUPS - d, 0) + bs, bs)
            qs = jnp.where(sub < GROUPS - d, qs * pltpu.roll(qs, GROUPS - d, 0), qs)
        enter.append(jnp.where(sub == 0, h, pltpu.roll(hs, 1, 0)))
        enter_back.append(jnp.where(sub == GROUPS - 1, b, pltpu.roll(bs, GROUPS - 1, 0)))

    def ahead(k, carry):
        new = []
        for r in range(rows):
            at = pl.ds(pl.multiple_of(r * steps + k * GROUPS, GROUPS), GROUPS)
            prev[at, :] = carry[r]
            h = a_in[at, :] * carry[r] + c_in[at, :] * xp[at, :]
            ggs[at, :] = gg_in[at, :] * h
            new.append(h)
        return tuple(new)

    lax.fori_loop(0, inner, ahead, tuple(enter), unroll=4)

    def back(i, carry):
        k = inner - 1 - i
        new = []
        for r in range(rows):
            at = pl.ds(pl.multiple_of(r * steps + k * GROUPS, GROUPS), GROUPS)
            adjoint = gh_in[at, :] + carry[r]
            new.append(a_in[at, :] * adjoint)
            gds[at, :] = adjoint * f_in[at, :] * (ru_in[at, :] - prev[at, :])
            gis[at, :] = adjoint * q_in[at, :]
            direct[at, :] = adjoint * c_in[at, :]
        return tuple(new)

    lax.fori_loop(0, inner, back, tuple(enter_back), unroll=4)
    unmove = jnp.where(order(tokens, steps, True), 1.0, 0.0).astype(BF16)
    gate_grad[...] = dot(unmove, ggs[...].astype(BF16)).astype(BF16)
    other = lax.axis_index("dp") % 2 == 0
    for half, value in enumerate((gds, gis)):
        grads[half] = value[...].astype(BF16)
        sent[half] = jnp.where(other, value[:, LANES:], value[:, :LANES])


def turn_kernel(x_own, x_other, out):
    tokens, model = x_own.shape
    part = model // (SIDE * SIDE)
    core = lax.axis_index("dp") % 2
    my_x, my_y = lax.axis_index("ctx") // SIDE, lax.axis_index("ctx") % SIDE
    for s, value in enumerate((x_own, x_other)):
        for bx in range(SIDE):
            turned = value[:, pl.ds(bx * SIDE * part, SIDE * part)].T.astype(BF16)
            for by in range(SIDE):
                dx, dy = (bx - my_x + SIDE) % SIDE, (by - my_y + SIDE) % SIDE
                place = jnp.where(core == 0, dx * SIDE + dy, dy * SIDE + dx)
                to = pl.ds(pl.multiple_of(place * part, part), part)
                out[to, pl.ds(s * tokens, tokens)] = turned[by * part : (by + 1) * part]


def weights_kernel(x_turned, grads, received, *rest):
    *outs, held = rest
    tokens = grads.shape[1]
    part = outs[0].shape[1]
    core = lax.axis_index("dp") % 2
    parts = grads.shape[2] // (2 * LANES)
    for half in range(2):
        for z in range(parts):
            to = pl.ds((half * parts + z) * LANES, LANES)
            own = jnp.where(
                core == 0,
                grads[half, :, pl.ds(2 * z * LANES, LANES)].astype(F32),
                grads[half, :, pl.ds((2 * z + 1) * LANES, LANES)].astype(F32),
            )
            held[pl.ds(0, tokens), to] = own.astype(BF16)
            held[pl.ds(tokens, tokens), to] = received[
                half, :, pl.ds(z * LANES, LANES)
            ].astype(BF16)
    for out, start in zip(outs, PIECES):
        span = out.shape[0] * part
        value = dot(x_turned[pl.ds(start * part, span), :], held[...])
        out[...] = value.reshape(out.shape)


def fold_kernel(own, low, low_more, high, high_more, *outs):
    for i, out in enumerate(outs):
        first, second = (low, low_more) if i < 2 else (high, high_more)
        out[...] = own[i] + first[i % 2] + second[i % 2]


def inputs_kernel(steps, grads, direct, weights, out):
    width = grads.shape[2]
    tokens = direct.shape[0]
    total = direct[...]
    for half in range(2):
        total = total + dot(
            grads[half], weights[:, half * width : (half + 1) * width], ((1,), (1,))
        )
    unmove = jnp.where(order(tokens, steps, True), 1.0, 0.0).astype(BF16)
    out[...] = dot(unmove, total.astype(BF16)).astype(BF16)


def sum_kernel(*refs):
    parts, outs = refs[:SIDE], refs[SIDE:]
    chips = len(outs)
    chip = lax.axis_index("dp") // 2
    for j, out in enumerate(outs):
        at = pl.ds(pl.multiple_of(lax.rem(chip + j, chips) * LANES, LANES), LANES)
        total = parts[0][:, at]
        for value in parts[1:]:
            total = total + value[:, at]
        out[...] = total


def params(mib):
    return pltpu.CompilerParams(vmem_limit_bytes=mib << 20)


def full(shape):
    return pl.BlockSpec(shape, lambda j: (0,) * len(shape))


def columns(rows, width=BLOCK, first=0):
    return pl.BlockSpec((rows, width), lambda j: (0, j + first))


def far(value):
    return pltpu.with_memory_space_constraint(value, pltpu.HBM)


def shaped(shape, dtype=F32):
    return jax.ShapeDtypeStruct(shape, dtype)


def per_device(
    inputs, gate_in, cotangent, recon_mask, segment_starts, weights, gate_bias, decay_rate
):
    rows, steps, model = inputs.shape
    tokens = rows * steps
    peers, pairs = lax.axis_size("ctx"), lax.axis_size("dp")
    chips = pairs // 2
    blocks = model // BLOCK
    flat = lambda value: value.reshape(tokens, model)
    bias = gate_bias.reshape(1, 2 * model)
    big = shaped((tokens, model))
    tile = columns(tokens)
    outs = pl.pallas_call(
        gates_kernel,
        grid=(blocks,),
        in_specs=[
            pl.BlockSpec(memory_space=pltpu.SMEM),
            full((tokens, model)),
            tile,
            tile,
            full((rows, steps)),
            columns(model),
            columns(model, first=blocks),
            columns(1),
            columns(1, first=blocks),
            columns(1),
        ],
        out_specs=[
            pl.BlockSpec((peers, 3 * rows, BLOCK), lambda j: (0, 0, j)),
            columns(3 * rows * GROUPS),
        ]
        + [tile] * 7
        + [full((tokens, model))],
        out_shape=[shaped((peers, 3 * rows, model)), shaped((3 * rows * GROUPS, model))] + [pltpu.HBM((tokens, model), F32)] * 7 + [big],
        scratch_shapes=[
            pltpu.VMEM((tokens, tokens), BF16),
            pltpu.VMEM((tokens, tokens), BF16),
            pltpu.VMEM((tokens, model), BF16),
        ]
        + [pltpu.VMEM((tokens, BLOCK), F32)] * 4,
        compiler_params=params(16),
        name="gates",
    )(
        segment_starts, far(flat(inputs)), far(flat(gate_in)), far(flat(cotangent)), far(recon_mask),
        far(weights), far(weights), far(bias), far(bias), far(decay_rate.reshape(1, model)),
    )
    summary, grouped, *middle, xp = outs
    middle = [far(v) for v in middle]
    swap = [(i, i ^ 1) for i in range(pairs)]
    x_other = lax.ppermute(xp, "dp", swap)
    slabs = lax.all_to_all(summary, "ctx", 0, 0, tiled=True)
    part = model // peers
    x_turned = pl.pallas_call(
        turn_kernel,
        out_shape=shaped((model, 2 * tokens), BF16),
        compiler_params=params(8),
        name="turn",
    )(xp, x_other)
    slabs, x_turned = lax.optimization_barrier((slabs, x_turned))
    pair_tile = pl.BlockSpec((2, tokens, BLOCK), lambda j: (0, 0, j))
    gate_grad, grads, sent, direct = pl.pallas_call(
        grads_kernel,
        grid=(blocks,),
        in_specs=[
            pl.BlockSpec((peers, 3 * rows, BLOCK), lambda j: (0, 0, j)),
            columns(3 * rows * GROUPS),
        ]
        + [tile] * 8,
        out_specs=[
            tile,
            pair_tile,
            pl.BlockSpec((2, tokens, LANES), lambda j: (0, 0, j)),
            tile,
        ],
        out_shape=[
            shaped((tokens, model), BF16),
            shaped((2, tokens, model), BF16),
            shaped((2, tokens, model // 2)),
            pltpu.HBM((tokens, model), F32),
        ],
        scratch_shapes=[pltpu.VMEM((tokens, BLOCK), F32)] * 4,
        compiler_params=params(12),
        name="grads",
    )(slabs, grouped, *middle, xp)
    direct = far(direct)
    received = lax.ppermute(sent, "dp", swap)
    piece = shaped((2, part, model))
    on2, back2, on1, back1, on_last, back_last, stay = pl.pallas_call(
        weights_kernel,
        out_shape=[piece] * 6 + [shaped((SIDE, part, model))],
        scratch_shapes=[pltpu.VMEM((2 * tokens, model), BF16)],
        compiler_params=params(16),
        name="weights",
    )(x_turned, grads, received)

    def move(value, step, first):
        pairs_of = []
        for i in range(peers * pairs):
            x, y, d = i // pairs // SIDE, i // pairs % SIDE, i % pairs
            if (d % 2 == 0) == first:
                x = (x + step) % SIDE
            else:
                y = (y + step) % SIDE
            pairs_of.append((i, (x * SIDE + y) * pairs + d))
        return lax.ppermute(value, ("ctx", "dp"), pairs_of)

    came_on2, came_back2 = move(on2, 1, True), move(back2, -1, True)
    came_on1, came_back1 = move(on1, 1, True), move(back1, -1, True)
    input_grad = pl.pallas_call(
        lambda *refs: inputs_kernel(steps, *refs),
        grid=(blocks,),
        in_specs=[
            full((2, tokens, model)),
            tile,
            pl.BlockSpec((BLOCK, 2 * model), lambda j: (j, 0)),
        ],
        out_specs=tile,
        out_shape=shaped((tokens, model), BF16),
        compiler_params=params(12),
        cost_estimate=pl.CostEstimate(
            flops=4 * tokens * model * model, bytes_accessed=6 * model * model, transcendentals=0
        ),
        name="inputs",
    )(grads, direct, far(weights))
    came_on2, came_back2, input_grad = lax.optimization_barrier((came_on2, came_back2, input_grad))
    came_on = move(on_last + came_on2, 1, True)
    came_back = move(back_last + came_back2, -1, True)
    near = shaped((part, model))
    quarters = pl.pallas_call(
        fold_kernel,
        out_shape=[near] * SIDE,
        compiler_params=params(8),
        name="fold",
    )(stay, came_back1, came_on, came_on1, came_back)
    others = [move(quarters[d], d, False) for d in (2, 1, 3)]
    by_chip = pl.pallas_call(
        sum_kernel,
        out_shape=[shaped((part, LANES))] * chips,
        compiler_params=params(4),
        name="slab_sum",
    )(quarters[0], *others)
    total = by_chip[0]
    for d in range(1, chips):
        hop = [(i, ((i // 2 + d) % chips) * 2 + i % 2) for i in range(pairs)]
        total = total + lax.ppermute(by_chip[d], "dp", hop)
    scale = 1.0 / math.sqrt(rows * pairs * steps * peers)
    return (
        input_grad.reshape(inputs.shape),
        gate_grad.reshape(inputs.shape),
        total * scale,
    )


def solution(mesh):
    return jax.shard_map(
        per_device,
        mesh=mesh,
        in_specs=(
            P("dp", "ctx", None),
            P("dp", "ctx", None),
            P("dp", "ctx", None),
            P("dp", "ctx"),
            P("dp", None),
            P(),
            P(),
            P(),
        ),
        out_specs=(P("dp", "ctx", None), P("dp", "ctx", None), P("ctx", "dp")),
        check_vma=False,
    )
```

```python
import math

import jax
import jax.numpy as jnp
from jax import lax
from jax.experimental import pallas as pl
from jax.experimental.pallas import tpu as pltpu
from jax.sharding import PartitionSpec as P

GROUPS = 8
LANES = 128
BLOCK = 256
F32 = jnp.float32
BF16 = jnp.bfloat16
ROOT = math.sqrt(2.0 / math.pi)
CUBIC = 0.044715
SIDE = 4
UNROLL = (16, 16, 16, 16)
PARAMS = (28, 28)
PIECES = (8, 10, 6, 12, 4, 14, 0)


def dot(a, b, dims=((1,), (0,))):
    return lax.dot_general(a, b, (dims, ((), ())), preferred_element_type=F32)


def order(tokens, steps, transpose=False):
    inner = steps // GROUPS
    rho = lax.broadcasted_iota(jnp.int32, (tokens, tokens), 1 if transpose else 0)
    at = lax.broadcasted_iota(jnp.int32, (tokens, tokens), 0 if transpose else 1)
    place = rho % steps
    source = (rho - place) + (place % GROUPS) * inner + place // GROUPS
    return at == source


def wide(value, width):
    return jnp.concatenate([value] * (width // value.shape[1]), axis=1)


def logistic(value):
    return 0.5 * jnp.tanh(0.5 * value) + 0.5


def gates_kernel(
    starts, x, gin, cot, mask, w_decay, w_input, bias, rate,
    summary, grouped, middle, xp_out,
    move, move_masked, xb, p1, p2, gins, gos,
):
    tokens, steps = x.shape[0], mask.shape[1]
    rows, inner = tokens // steps, steps // GROUPS
    width = gin.shape[1]
    block = pl.program_id(0)
    me = lax.axis_index("ctx")
    base = me * steps
    lanes = pl.ds(pl.multiple_of(block * width, width), width)
    lanes_input = pl.ds(pl.multiple_of(x.shape[1] + block * width, width), width)

    @pl.when(block == 0)
    def _():
        hit = order(tokens, steps)
        masks = mask[...].astype(F32)
        mask_row = jnp.concatenate([masks[r : r + 1] for r in range(rows)], axis=1)
        move[...] = jnp.where(hit, 1.0, 0.0).astype(BF16)
        move_masked[...] = jnp.where(hit, jnp.broadcast_to(mask_row, hit.shape), 0.0).astype(BF16)
        xp_out[...] = dot(move[...], x[...])
        xb[...] = xp_out[...].astype(BF16)

    p1[...] = dot(xb[...], w_decay[...]) + bias[:, lanes]
    p2[...] = dot(xb[...], w_input[...]) + bias[:, lanes_input]
    gins[...] = dot(move[...], gin[...])
    gos[...] = dot(move_masked[...], cot[...])
    rate8 = jnp.broadcast_to(8.0 * rate[:, lanes], (GROUPS, width))
    spot = lax.broadcasted_iota(jnp.int32, (GROUPS, LANES), 0) * inner + base
    spots = [
        [jnp.broadcast_to(starts[r : r + 1, s : s + 1], spot.shape) for s in range(starts.shape[1])]
        for r in range(rows)
    ]

    def ahead(k, carry):
        new = []
        for r in range(rows):
            h, prod = carry[2 * r], carry[2 * r + 1]
            at = pl.ds(pl.multiple_of(r * steps + k * GROUPS, GROUPS), GROUPS)
            here = spot + k
            reset = here == 0
            for s in range(starts.shape[1]):
                reset = reset | (here == spots[r][s])
            keep = wide(jnp.where(reset, 0.0, 1.0), width)
            gate_decay = logistic(p1[at, :])
            gate_input = logistic(p2[at, :])
            xt = xp_out[at, lanes]
            arg = rate8 * gate_decay
            y = 2.0 * arg
            step = jnp.exp(-arg)
            square = y * (
                1.0 - y * (1 / 2 - y * (1 / 6 - y * (1 / 24 - y * (1 / 120 - y * (1 / 720)))))
            )
            a = keep * step
            c = ((1.0 - keep) + keep * jnp.sqrt(square)) * gate_input
            u = c * xt
            ratio = 0.5 + y * (0.25 + y * (1 / 24 - (y * y) * (1 / 1440)))
            middle[0, at, lanes] = a
            middle[1, at, lanes] = c
            middle[2, at, lanes] = (1.0 - gate_decay) * arg * a
            middle[3, at, lanes] = a * ratio * u
            middle[4, at, lanes] = u * (1.0 - gate_input)
            new += [a * h + u, a * prod]
            g, go = gins[at, :], gos[at, :]
            gsq = g * g
            th = jnp.tanh(ROOT * g * (1.0 + CUBIC * gsq))
            half = 0.5 * (1.0 + th)
            middle[5, at, lanes] = go * (g * half)
            middle[6, at, lanes] = go * (
                half + 0.5 * g * (1.0 - th * th) * (ROOT * (1.0 + (3.0 * CUBIC) * gsq))
            )
        return tuple(new)

    zero = jnp.zeros((GROUPS, width), F32)
    one = jnp.ones((GROUPS, width), F32)
    forward = lax.fori_loop(0, inner, ahead, (zero, one) * rows, unroll=UNROLL[0])

    def back(i, carry):
        k = inner - 1 - i
        new = []
        for r in range(rows):
            at = pl.ds(pl.multiple_of(r * steps + k * GROUPS, GROUPS), GROUPS)
            new.append(middle[0, at, lanes] * (middle[5, at, lanes] + carry[r]))
        return tuple(new)

    backward = lax.fori_loop(0, inner, back, (zero,) * rows, unroll=UNROLL[1])

    for r in range(rows):
        hs, ps, bs = forward[2 * r], forward[2 * r + 1], backward[r]
        grouped[pl.ds((0 * rows + r) * GROUPS, GROUPS), lanes] = ps
        grouped[pl.ds((1 * rows + r) * GROUPS, GROUPS), lanes] = hs
        grouped[pl.ds((2 * rows + r) * GROUPS, GROUPS), lanes] = bs
        qs = ps
        for d in (1, 2, 4):
            hs = ps * pltpu.roll(hs, d, 0) + hs
            ps = ps * pltpu.roll(ps, d, 0)
            bs = qs * pltpu.roll(bs, GROUPS - d, 0) + bs
            qs = qs * pltpu.roll(qs, GROUPS - d, 0)
        for i in range(summary.shape[0]):
            summary[i, r : r + 1, :] = ps[GROUPS - 1 :]
            summary[i, rows + r : rows + r + 1, :] = jnp.where(me < i, hs[GROUPS - 1 :], bs[:1])


def grads_kernel(
    slabs, grouped, middle, xp,
    gate_grad, grads, sent, direct,
    prev, ggs, gds, gis,
):
    count = slabs.shape[0]
    rows = slabs.shape[1] // 2
    tokens, width = gate_grad.shape
    lanes = pl.ds(pl.multiple_of(pl.program_id(0) * width, width), width)
    to_send = pl.ds(pl.multiple_of(pl.program_id(0) * LANES, LANES), LANES)
    steps = tokens // rows
    inner = steps // GROUPS
    me = lax.axis_index("ctx")
    sub = lax.broadcasted_iota(jnp.int32, (GROUPS, width), 0)

    def spread(i, row):
        return jnp.broadcast_to(slabs[i, row : row + 1, lanes], (GROUPS, width))

    enter, enter_back = [], []
    for r in range(rows):
        h = jnp.zeros((GROUPS, width), F32)
        for i in range(count - 1):
            h = jnp.where(i < me, spread(i, r) * h + spread(i, rows + r), h)
        b = jnp.zeros((GROUPS, width), F32)
        for i in range(count - 1, 0, -1):
            b = jnp.where(i > me, spread(i, r) * b + spread(i, rows + r), b)
        ps = grouped[pl.ds((0 * rows + r) * GROUPS, GROUPS), lanes]
        hs = grouped[pl.ds((1 * rows + r) * GROUPS, GROUPS), lanes]
        bs = grouped[pl.ds((2 * rows + r) * GROUPS, GROUPS), lanes]
        hs = jnp.where(sub == 0, ps * h + hs, hs)
        bs = jnp.where(sub == GROUPS - 1, ps * b + bs, bs)
        qs = ps
        for d in (1, 2, 4):
            hs = jnp.where(sub >= d, ps * pltpu.roll(hs, d, 0) + hs, hs)
            ps = jnp.where(sub >= d, ps * pltpu.roll(ps, d, 0), ps)
            bs = jnp.where(sub < GROUPS - d, qs * pltpu.roll(bs, GROUPS - d, 0) + bs, bs)
            qs = jnp.where(sub < GROUPS - d, qs * pltpu.roll(qs, GROUPS - d, 0), qs)
        enter.append(jnp.where(sub == 0, h, pltpu.roll(hs, 1, 0)))
        enter_back.append(jnp.where(sub == GROUPS - 1, b, pltpu.roll(bs, GROUPS - 1, 0)))

    def ahead(k, carry):
        new = []
        for r in range(rows):
            at = pl.ds(pl.multiple_of(r * steps + k * GROUPS, GROUPS), GROUPS)
            prev[at, :] = carry[r]
            h = middle[0, at, lanes] * carry[r] + middle[1, at, lanes] * xp[at, lanes]
            ggs[at, :] = middle[6, at, lanes] * h
            new.append(h)
        return tuple(new)

    lax.fori_loop(0, inner, ahead, tuple(enter), unroll=UNROLL[2])

    def back(i, carry):
        k = inner - 1 - i
        new = []
        for r in range(rows):
            at = pl.ds(pl.multiple_of(r * steps + k * GROUPS, GROUPS), GROUPS)
            adjoint = middle[5, at, lanes] + carry[r]
            new.append(middle[0, at, lanes] * adjoint)
            gds[at, :] = adjoint * middle[2, at, lanes] * (middle[3, at, lanes] - prev[at, :])
            gis[at, :] = adjoint * middle[4, at, lanes]
            direct[at, lanes] = adjoint * middle[1, at, lanes]
        return tuple(new)

    lax.fori_loop(0, inner, back, tuple(enter_back), unroll=UNROLL[3])
    unmove = jnp.where(order(tokens, steps, True), 1.0, 0.0).astype(BF16)
    gate_grad[...] = dot(unmove, ggs[...].astype(BF16)).astype(BF16)
    other = lax.axis_index("dp") % 2 == 0
    for half, value in enumerate((gds, gis)):
        grads[half, :, lanes] = value[...].astype(BF16)
        sent[half, :, to_send] = jnp.where(other, value[:, LANES:], value[:, :LANES])


def turn_kernel(steps, x_own, x_other, out):
    tokens, model = x_own.shape
    part = model // (SIDE * SIDE)
    core = lax.axis_index("dp") % 2
    my_x, my_y = lax.axis_index("ctx") // SIDE, lax.axis_index("ctx") % SIDE
    place = jnp.where(order(tokens, steps), 1.0, 0.0).astype(BF16)
    for s, value in enumerate((x_own, x_other)):
        for bx in range(SIDE):
            turned = value[:, pl.ds(bx * SIDE * part, SIDE * part)]
            if s == 1:
                turned = dot(place, turned.astype(BF16))
            turned = turned.T.astype(BF16)
            for by in range(SIDE):
                dx, dy = (bx - my_x + SIDE) % SIDE, (by - my_y + SIDE) % SIDE
                block = jnp.where(core == 0, dx * SIDE + dy, dy * SIDE + dx)
                to = pl.ds(pl.multiple_of(block * part, part), part)
                out[to, pl.ds(s * tokens, tokens)] = turned[by * part : (by + 1) * part]


def pieces(x_turned, held, outs, starts):
    part = outs[0].shape[1]
    for out, start in zip(outs, starts):
        value = dot(x_turned[pl.ds(start * part, out.shape[0] * part), :], held[...])
        out[...] = value.reshape(out.shape)


def first_weights_kernel(x_turned, grads, received, held, *outs):
    tokens = grads.shape[1]
    core = lax.axis_index("dp") % 2
    parts = grads.shape[2] // (2 * LANES)
    for half in range(2):
        for z in range(parts):
            to = pl.ds((half * parts + z) * LANES, LANES)
            own = jnp.where(
                core == 0,
                grads[half, :, pl.ds(2 * z * LANES, LANES)].astype(F32),
                grads[half, :, pl.ds((2 * z + 1) * LANES, LANES)].astype(F32),
            )
            held[pl.ds(0, tokens), to] = own.astype(BF16)
            held[pl.ds(tokens, tokens), to] = received[
                half, :, pl.ds(z * LANES, LANES)
            ].astype(BF16)
    pieces(x_turned, held, outs, PIECES[:2])


def more_weights_kernel(x_turned, held, *outs):
    pieces(x_turned, held, outs, PIECES[2:])


def fold_kernel(own, low, low_more, high, high_more, *outs):
    for i, out in enumerate(outs):
        first, second = (low, low_more) if i < 2 else (high, high_more)
        out[...] = own[i] + first[i % 2] + second[i % 2]


def inputs_kernel(steps, grads, direct, weights, out):
    width = grads.shape[2]
    tokens = direct.shape[0]
    total = direct[...]
    for half in range(2):
        total = total + dot(
            grads[half], weights[:, half * width : (half + 1) * width], ((1,), (1,))
        )
    unmove = jnp.where(order(tokens, steps, True), 1.0, 0.0).astype(BF16)
    out[...] = dot(unmove, total.astype(BF16)).astype(BF16)


def sum_kernel(scale, *refs):
    *parts, out = refs
    for z in range(out.shape[0]):
        at = pl.ds(z * LANES, LANES)
        total = parts[0][:, at]
        for value in parts[1:]:
            total = total + value[:, at]
        out[z] = total * scale


def params(mib):
    return pltpu.CompilerParams(vmem_limit_bytes=mib << 20)


def full(shape):
    return pl.BlockSpec(shape, lambda j: (0,) * len(shape))


def columns(rows, width=BLOCK, first=0):
    return pl.BlockSpec((rows, width), lambda j: (0, j + first))


def far(value):
    return pltpu.with_memory_space_constraint(value, pltpu.HBM)


def shaped(shape, dtype=F32):
    return jax.ShapeDtypeStruct(shape, dtype)


def gates(
    inputs, gate_in, cotangent, recon_mask, segment_starts, weights, gate_bias, decay_rate, peers
):
    rows, steps, model = inputs.shape
    tokens = rows * steps
    blocks = model // BLOCK
    flat = lambda value: value.reshape(tokens, model)
    bias = gate_bias.reshape(1, 2 * model)
    tile = columns(tokens)
    near = pl.BlockSpec(memory_space=pltpu.VMEM)
    return pl.pallas_call(
        gates_kernel,
        grid=(blocks,),
        in_specs=[
            full(segment_starts.shape),
            full((tokens, model)),
            tile,
            tile,
            full((rows, steps)),
            columns(model),
            columns(model, first=blocks),
            full((1, 2 * model)),
            full((1, model)),
        ],
        out_specs=[pl.BlockSpec((peers, 2 * rows, BLOCK), lambda j: (0, 0, j)), near, near, near],
        out_shape=[
            shaped((peers, 2 * rows, model)),
            pltpu.VMEM((3 * rows * GROUPS, model), F32),
            pltpu.VMEM((7, tokens, model), F32),
            pltpu.VMEM((tokens, model), F32),
        ],
        scratch_shapes=[
            pltpu.VMEM((tokens, tokens), BF16),
            pltpu.VMEM((tokens, tokens), BF16),
            pltpu.VMEM((tokens, model), BF16),
        ]
        + [pltpu.VMEM((tokens, BLOCK), F32)] * 4,
        compiler_params=params(PARAMS[0]),
        name="gates",
    )(
        far(segment_starts), far(flat(inputs)), far(flat(gate_in)), far(flat(cotangent)), far(recon_mask),
        far(weights), far(weights), far(bias), far(decay_rate.reshape(1, model)),
    )


def gradients(slabs, grouped, middle, xp):
    tokens, model = xp.shape
    near = pl.BlockSpec(memory_space=pltpu.VMEM)
    return pl.pallas_call(
        grads_kernel,
        grid=(model // BLOCK,),
        in_specs=[near] * 4,
        out_specs=[columns(tokens), near, near, near],
        out_shape=[
            shaped((tokens, model), BF16),
            pltpu.VMEM((2, tokens, model), BF16),
            pltpu.VMEM((2, tokens, model // 2), F32),
            pltpu.VMEM((tokens, model), F32),
        ],
        scratch_shapes=[pltpu.VMEM((tokens, BLOCK), F32)] * 4,
        compiler_params=params(PARAMS[1]),
        name="grads",
    )(slabs, grouped, middle, xp)


def input_gradient(grads, direct, weights, steps):
    tokens, model = direct.shape
    return pl.pallas_call(
        lambda *refs: inputs_kernel(steps, *refs),
        grid=(model // BLOCK,),
        in_specs=[
            full((2, tokens, model)),
            columns(tokens),
            pl.BlockSpec((BLOCK, 2 * model), lambda j: (j, 0)),
        ],
        out_specs=columns(tokens),
        out_shape=shaped((tokens, model), BF16),
        compiler_params=params(12),
        cost_estimate=pl.CostEstimate(
            flops=4 * tokens * model * model, bytes_accessed=6 * model * model, transcendentals=0
        ),
        name="inputs",
    )(grads, direct, far(weights))


def per_device(
    inputs, gate_in, cotangent, recon_mask, segment_starts, weights, gate_bias, decay_rate
):
    rows, steps, model = inputs.shape
    tokens = rows * steps
    peers, pairs = lax.axis_size("ctx"), lax.axis_size("dp")
    chips = pairs // 2
    swap = [(i, i ^ 1) for i in range(pairs)]
    x_other = lax.ppermute(inputs.reshape(tokens, model).astype(F32), "dp", swap)
    summary, grouped, middle, xp = gates(
        inputs, gate_in, cotangent, recon_mask, segment_starts, weights, gate_bias, decay_rate, peers
    )
    summary, x_other = lax.optimization_barrier((summary, x_other))
    slabs = lax.all_to_all(summary, "ctx", 0, 0, tiled=True)
    part = model // peers
    gate_grad, grads, sent, direct = gradients(slabs, grouped, middle, xp)
    received = lax.ppermute(sent, "dp", swap)
    x_turned = pl.pallas_call(
        lambda *refs: turn_kernel(steps, *refs),
        out_shape=shaped((model, 2 * tokens), BF16),
        compiler_params=params(8),
        name="turn",
    )(xp, x_other)
    piece = shaped((2, part, model))
    held, on2, back2 = pl.pallas_call(
        first_weights_kernel,
        out_shape=[shaped((2 * tokens, model), BF16), piece, piece],
        compiler_params=params(12),
        name="first_weights",
    )(x_turned, grads, received)
    on1, back1, on_last, back_last, stay = pl.pallas_call(
        more_weights_kernel,
        out_shape=[piece] * 4 + [shaped((SIDE, part, model))],
        compiler_params=params(12),
        name="more_weights",
    )(x_turned, held)

    def move(value, step, first):
        pairs_of = []
        for i in range(peers * pairs):
            x, y, d = i // pairs // SIDE, i // pairs % SIDE, i % pairs
            if (d % 2 == 0) == first:
                x = (x + step) % SIDE
            else:
                y = (y + step) % SIDE
            pairs_of.append((i, (x * SIDE + y) * pairs + d))
        return lax.ppermute(value, ("ctx", "dp"), pairs_of)

    came_on2, came_back2 = move(on2, 1, True), move(back2, -1, True)
    came_on1, came_back1 = move(on1, 1, True), move(back1, -1, True)
    came_on1, came_back1, direct = lax.optimization_barrier((came_on1, came_back1, direct))
    came_on = move(on_last + came_on2, 1, True)
    came_back = move(back_last + came_back2, -1, True)
    input_grad = input_gradient(grads, direct, weights, steps)
    came_on, came_back, input_grad = lax.optimization_barrier((came_on, came_back, input_grad))
    scale = 1.0 / math.sqrt(rows * pairs * steps * peers)
    near = shaped((part, model))
    quarters = pl.pallas_call(
        fold_kernel,
        out_shape=[near] * SIDE,
        compiler_params=params(8),
        name="fold",
    )(stay, came_back1, came_on, came_on1, came_back)
    others = [move(quarters[d], d, False) for d in (2, 1, 3)]
    by_chip = pl.pallas_call(
        lambda *refs: sum_kernel(scale, *refs),
        out_shape=shaped((chips, part, LANES)),
        compiler_params=params(4),
        name="slab_sum",
    )(quarters[0], *others)
    same_core = [list(range(core, pairs, 2)) for core in range(2)]
    by_chip = lax.all_to_all(
        by_chip, "dp", 0, 0, axis_index_groups=same_core, tiled=True
    )
    total = jnp.sum(by_chip, axis=0)
    return (
        input_grad.reshape(inputs.shape),
        gate_grad.reshape(inputs.shape),
        total,
    )


def solution(mesh):
    return jax.shard_map(
        per_device,
        mesh=mesh,
        in_specs=(
            P("dp", "ctx", None),
            P("dp", "ctx", None),
            P("dp", "ctx", None),
            P("dp", "ctx"),
            P("dp", None),
            P(),
            P(),
            P(),
        ),
        out_specs=(P("dp", "ctx", None), P("dp", "ctx", None), P("ctx", "dp")),
        check_vma=False,
    )
```

```python
import math

import jax
import jax.numpy as jnp
from jax import lax
from jax.experimental import pallas as pl
from jax.experimental.pallas import tpu as pltpu
from jax.sharding import PartitionSpec as P

GROUPS = 8
LANES = 128
BLOCK = 256
F32 = jnp.float32
BF16 = jnp.bfloat16
ROOT = math.sqrt(2.0 / math.pi)
CUBIC = 0.044715
SIDE = 4
WIDE = 512
WIDTH = 512
UNROLL = (16, 16, 16, 16)
PARAMS = (28, 28)
PIECES = (8, 10, 6, 12, 4, 14, 0)


def dot(a, b, dims=((1,), (0,))):
    return lax.dot_general(a, b, (dims, ((), ())), preferred_element_type=F32)


def order(tokens, steps, transpose=False):
    inner = steps // GROUPS
    shift, mask = GROUPS.bit_length() - 1, steps - 1
    rho = lax.broadcasted_iota(jnp.int32, (tokens, tokens), 1 if transpose else 0)
    at = lax.broadcasted_iota(jnp.int32, (tokens, tokens), 0 if transpose else 1)
    place = rho & mask
    source = (rho - place) + (place & (GROUPS - 1)) * inner + (place >> shift)
    return at == source


def wide(value, width):
    return jnp.concatenate([value] * (width // value.shape[1]), axis=1)


def logistic(value):
    return 0.5 * jnp.tanh(0.5 * value) + 0.5


def gates_kernel(
    starts, x, gin, cot, mask, w_decay, w_input, bias, rate,
    summary, grouped, middle, xp_out,
    move, move_masked, xb, p1, p2, gins, gos,
):
    tokens, steps = x.shape[0], mask.shape[1]
    rows, inner = tokens // steps, steps // GROUPS
    width = gin.shape[1]
    block = pl.program_id(0)
    me = lax.axis_index("ctx")
    base = me * steps
    lanes = pl.ds(pl.multiple_of(block * width, width), width)
    lanes_input = pl.ds(pl.multiple_of(x.shape[1] + block * width, width), width)

    @pl.when(block == 0)
    def _():
        hit = order(tokens, steps)
        masks = mask[...].astype(F32)
        mask_row = jnp.concatenate([masks[r : r + 1] for r in range(rows)], axis=1)
        move[...] = jnp.where(hit, 1.0, 0.0).astype(BF16)
        move_masked[...] = jnp.where(hit, jnp.broadcast_to(mask_row, hit.shape), 0.0).astype(BF16)
        xp_out[...] = dot(move[...], x[...])
        xb[...] = xp_out[...].astype(BF16)

    p1[...] = dot(xb[...], w_decay[...]) + bias[:, lanes]
    p2[...] = dot(xb[...], w_input[...]) + bias[:, lanes_input]
    gins[...] = dot(move[...], gin[...])
    gos[...] = dot(move_masked[...], cot[...])
    rate8 = jnp.broadcast_to(8.0 * rate[:, lanes], (GROUPS, width))
    spot = lax.broadcasted_iota(jnp.int32, (GROUPS, LANES), 0) * inner + base
    spots = [
        [jnp.broadcast_to(starts[r : r + 1, s : s + 1], spot.shape) for s in range(starts.shape[1])]
        for r in range(rows)
    ]

    def ahead(k, carry):
        new = []
        for r in range(rows):
            h, prod = carry[2 * r], carry[2 * r + 1]
            at = pl.ds(pl.multiple_of(r * steps + k * GROUPS, GROUPS), GROUPS)
            here = spot + k
            reset = here == 0
            for s in range(starts.shape[1]):
                reset = reset | (here == spots[r][s])
            keep = wide(jnp.where(reset, 0.0, 1.0), width)
            gate_decay = logistic(p1[at, :])
            gate_input = logistic(p2[at, :])
            xt = xp_out[at, lanes]
            arg = rate8 * gate_decay
            y = 2.0 * arg
            step = jnp.exp(-arg)
            square = y * (
                1.0 - y * (1 / 2 - y * (1 / 6 - y * (1 / 24 - y * (1 / 120 - y * (1 / 720)))))
            )
            a = keep * step
            c = ((1.0 - keep) + keep * jnp.sqrt(square)) * gate_input
            u = c * xt
            ratio = 0.5 + y * (0.25 + y * (1 / 24 - (y * y) * (1 / 1440)))
            middle[0, at, lanes] = a
            middle[1, at, lanes] = c
            middle[2, at, lanes] = (1.0 - gate_decay) * arg * a
            middle[3, at, lanes] = a * ratio * u
            middle[4, at, lanes] = u * (1.0 - gate_input)
            new += [a * h + u, a * prod]
            g, go = gins[at, :], gos[at, :]
            gsq = g * g
            th = jnp.tanh(ROOT * g * (1.0 + CUBIC * gsq))
            half = 0.5 * (1.0 + th)
            middle[5, at, lanes] = go * (g * half)
            middle[6, at, lanes] = go * (
                half + 0.5 * g * (1.0 - th * th) * (ROOT * (1.0 + (3.0 * CUBIC) * gsq))
            )
        return tuple(new)

    zero = jnp.zeros((GROUPS, width), F32)
    one = jnp.ones((GROUPS, width), F32)
    forward = lax.fori_loop(0, inner, ahead, (zero, one) * rows, unroll=UNROLL[0])

    def back(i, carry):
        k = inner - 1 - i
        new = []
        for r in range(rows):
            at = pl.ds(pl.multiple_of(r * steps + k * GROUPS, GROUPS), GROUPS)
            new.append(middle[0, at, lanes] * (middle[5, at, lanes] + carry[r]))
        return tuple(new)

    backward = lax.fori_loop(0, inner, back, (zero,) * rows, unroll=UNROLL[1])

    for r in range(rows):
        hs, ps, bs = forward[2 * r], forward[2 * r + 1], backward[r]
        grouped[pl.ds((0 * rows + r) * GROUPS, GROUPS), lanes] = ps
        grouped[pl.ds((1 * rows + r) * GROUPS, GROUPS), lanes] = hs
        grouped[pl.ds((2 * rows + r) * GROUPS, GROUPS), lanes] = bs
        qs = ps
        for d in (1, 2, 4):
            hs = ps * pltpu.roll(hs, d, 0) + hs
            ps = ps * pltpu.roll(ps, d, 0)
            bs = qs * pltpu.roll(bs, GROUPS - d, 0) + bs
            qs = qs * pltpu.roll(qs, GROUPS - d, 0)
        for i in range(summary.shape[0]):
            summary[i, r : r + 1, :] = ps[GROUPS - 1 :]
            summary[i, rows + r : rows + r + 1, :] = jnp.where(me < i, hs[GROUPS - 1 :], bs[:1])


def grads_kernel(
    slabs, grouped, middle, xp,
    gate_grad, grads, sent, direct,
    prev, ggs, gds, gis,
):
    count = slabs.shape[0]
    rows = slabs.shape[1] // 2
    tokens, width = gate_grad.shape
    lanes = pl.ds(pl.multiple_of(pl.program_id(0) * width, width), width)
    to_send = pl.ds(pl.multiple_of(pl.program_id(0) * LANES, LANES), LANES)
    steps = tokens // rows
    inner = steps // GROUPS
    me = lax.axis_index("ctx")
    sub = lax.broadcasted_iota(jnp.int32, (GROUPS, width), 0)

    def spread(i, row):
        return jnp.broadcast_to(slabs[i, row : row + 1, lanes], (GROUPS, width))

    enter, enter_back = [], []
    for r in range(rows):
        h = jnp.zeros((GROUPS, width), F32)
        for i in range(count - 1):
            h = jnp.where(i < me, spread(i, r) * h + spread(i, rows + r), h)
        b = jnp.zeros((GROUPS, width), F32)
        for i in range(count - 1, 0, -1):
            b = jnp.where(i > me, spread(i, r) * b + spread(i, rows + r), b)
        ps = grouped[pl.ds((0 * rows + r) * GROUPS, GROUPS), lanes]
        hs = grouped[pl.ds((1 * rows + r) * GROUPS, GROUPS), lanes]
        bs = grouped[pl.ds((2 * rows + r) * GROUPS, GROUPS), lanes]
        hs = jnp.where(sub == 0, ps * h + hs, hs)
        bs = jnp.where(sub == GROUPS - 1, ps * b + bs, bs)
        qs = ps
        for d in (1, 2, 4):
            hs = jnp.where(sub >= d, ps * pltpu.roll(hs, d, 0) + hs, hs)
            ps = jnp.where(sub >= d, ps * pltpu.roll(ps, d, 0), ps)
            bs = jnp.where(sub < GROUPS - d, qs * pltpu.roll(bs, GROUPS - d, 0) + bs, bs)
            qs = jnp.where(sub < GROUPS - d, qs * pltpu.roll(qs, GROUPS - d, 0), qs)
        enter.append(jnp.where(sub == 0, h, pltpu.roll(hs, 1, 0)))
        enter_back.append(jnp.where(sub == GROUPS - 1, b, pltpu.roll(bs, GROUPS - 1, 0)))

    def ahead(k, carry):
        new = []
        for r in range(rows):
            at = pl.ds(pl.multiple_of(r * steps + k * GROUPS, GROUPS), GROUPS)
            prev[at, :] = carry[r]
            h = middle[0, at, lanes] * carry[r] + middle[1, at, lanes] * xp[at, lanes]
            ggs[at, :] = middle[6, at, lanes] * h
            new.append(h)
        return tuple(new)

    lax.fori_loop(0, inner, ahead, tuple(enter), unroll=UNROLL[2])

    def back(i, carry):
        k = inner - 1 - i
        new = []
        for r in range(rows):
            at = pl.ds(pl.multiple_of(r * steps + k * GROUPS, GROUPS), GROUPS)
            adjoint = middle[5, at, lanes] + carry[r]
            new.append(middle[0, at, lanes] * adjoint)
            gds[at, :] = adjoint * middle[2, at, lanes] * (middle[3, at, lanes] - prev[at, :])
            gis[at, :] = adjoint * middle[4, at, lanes]
            direct[at, lanes] = adjoint * middle[1, at, lanes]
        return tuple(new)

    lax.fori_loop(0, inner, back, tuple(enter_back), unroll=UNROLL[3])

    unmove = jnp.where(order(tokens, steps, True), 1.0, 0.0).astype(BF16)
    gate_grad[...] = dot(unmove, ggs[...].astype(BF16)).astype(BF16)
    other = lax.axis_index("dp") % 2 == 0
    for half, value in enumerate((gds, gis)):
        grads[half, :, lanes] = value[...].astype(BF16)
        sent[half, :, to_send] = jnp.where(other, value[:, LANES:], value[:, :LANES])


def turn_kernel(x_own, x_other, out):
    tokens, model = x_own.shape
    part = model // (SIDE * SIDE)
    core = lax.axis_index("dp") % 2
    my_x, my_y = lax.axis_index("ctx") // SIDE, lax.axis_index("ctx") % SIDE
    for s, value in enumerate((x_own, x_other)):
        for bx in range(SIDE):
            turned = value[:, pl.ds(bx * SIDE * part, SIDE * part)].T.astype(BF16)
            for by in range(SIDE):
                dx, dy = (bx - my_x + SIDE) % SIDE, (by - my_y + SIDE) % SIDE
                block = jnp.where(core == 0, dx * SIDE + dy, dy * SIDE + dx)
                to = pl.ds(pl.multiple_of(block * part, part), part)
                out[to, pl.ds(s * tokens, tokens)] = turned[by * part : (by + 1) * part]


def pieces(x_turned, held, outs, starts):
    part = outs[0].shape[1]
    for out, start in zip(outs, starts):
        value = dot(x_turned[pl.ds(start * part, out.shape[0] * part), :], held[...])
        out[...] = value.reshape(out.shape)


def first_weights_kernel(x_turned, grads, received, held, *outs):
    tokens = grads.shape[1]
    core = lax.axis_index("dp") % 2
    parts = grads.shape[2] // (2 * LANES)
    for half in range(2):
        for z in range(parts):
            to = pl.ds((half * parts + z) * LANES, LANES)
            own = jnp.where(
                core == 0,
                grads[half, :, pl.ds(2 * z * LANES, LANES)].astype(F32),
                grads[half, :, pl.ds((2 * z + 1) * LANES, LANES)].astype(F32),
            )
            held[pl.ds(0, tokens), to] = own.astype(BF16)
            held[pl.ds(tokens, tokens), to] = received[
                half, :, pl.ds(z * LANES, LANES)
            ].astype(BF16)
    pieces(x_turned, held, outs, PIECES[:2])


def more_weights_kernel(x_turned, held, *outs):
    pieces(x_turned, held, outs, PIECES[2:])


def fold_kernel(own, low, low_more, high, high_more, *outs):
    for i, out in enumerate(outs):
        first, second = (low, low_more) if i < 2 else (high, high_more)
        out[...] = own[i] + first[i % 2] + second[i % 2]


def inputs_kernel(steps, grads, direct, weights, out):
    model = direct.shape[1]
    tokens, width = out.shape
    at = pl.ds(pl.multiple_of(pl.program_id(0) * width, width), width)
    total = direct[:, at]
    for half in range(2):
        total = total + dot(
            grads[half], weights[at, pl.ds(half * model, model)], ((1,), (1,))
        )
    unmove = jnp.where(order(tokens, steps, True), 1.0, 0.0).astype(BF16)
    out[...] = dot(unmove, total.astype(BF16)).astype(BF16)


def sum_kernel(scale, *refs):
    *parts, out = refs
    for z in range(out.shape[0]):
        at = pl.ds(z * LANES, LANES)
        total = parts[0][:, at]
        for value in parts[1:]:
            total = total + value[:, at]
        out[z] = total * scale


def params(mib):
    return pltpu.CompilerParams(vmem_limit_bytes=mib << 20)


def full(shape):
    return pl.BlockSpec(shape, lambda j: (0,) * len(shape))


def columns(rows, width=BLOCK, first=0):
    return pl.BlockSpec((rows, width), lambda j: (0, j + first))


def far(value):
    return pltpu.with_memory_space_constraint(value, pltpu.HBM)


def shaped(shape, dtype=F32):
    return jax.ShapeDtypeStruct(shape, dtype)


def gates(
    inputs, gate_in, cotangent, recon_mask, segment_starts, weights, gate_bias, decay_rate, peers
):
    rows, steps, model = inputs.shape
    tokens = rows * steps
    blocks = model // WIDTH
    flat = lambda value: value.reshape(tokens, model)
    bias = gate_bias.reshape(1, 2 * model)
    tile = columns(tokens, WIDTH)
    near = pl.BlockSpec(memory_space=pltpu.VMEM)
    return pl.pallas_call(
        gates_kernel,
        grid=(blocks,),
        in_specs=[
            full(segment_starts.shape),
            full((tokens, model)),
            tile,
            tile,
            full((rows, steps)),
            columns(model, WIDTH),
            columns(model, WIDTH, blocks),
            full((1, 2 * model)),
            full((1, model)),
        ],
        out_specs=[pl.BlockSpec((peers, 2 * rows, WIDTH), lambda j: (0, 0, j)), near, near, near],
        out_shape=[
            shaped((peers, 2 * rows, model)),
            pltpu.VMEM((3 * rows * GROUPS, model), F32),
            pltpu.VMEM((7, tokens, model), F32),
            pltpu.VMEM((tokens, model), F32),
        ],
        scratch_shapes=[
            pltpu.VMEM((tokens, tokens), BF16),
            pltpu.VMEM((tokens, tokens), BF16),
            pltpu.VMEM((tokens, model), BF16),
        ]
        + [pltpu.VMEM((tokens, WIDTH), F32)] * 4,
        compiler_params=params(PARAMS[0]),
        name="gates",
    )(
        far(segment_starts), far(flat(inputs)), far(flat(gate_in)), far(flat(cotangent)), far(recon_mask),
        far(weights), far(weights), far(bias), far(decay_rate.reshape(1, model)),
    )


def gradients(slabs, grouped, middle, xp):
    tokens, model = xp.shape
    near = pl.BlockSpec(memory_space=pltpu.VMEM)
    return pl.pallas_call(
        grads_kernel,
        grid=(model // BLOCK,),
        in_specs=[near] * 4,
        out_specs=[columns(tokens), near, near, near],
        out_shape=[
            shaped((tokens, model), BF16),
            pltpu.VMEM((2, tokens, model), BF16),
            pltpu.VMEM((2, tokens, model // 2), F32),
            pltpu.VMEM((tokens, model), F32),
        ],
        scratch_shapes=[pltpu.VMEM((tokens, BLOCK), F32)] * 4,
        compiler_params=params(PARAMS[1]),
        name="grads",
    )(slabs, grouped, middle, xp)


def input_gradient(grads, direct, weights, steps):
    tokens, model = direct.shape
    near = pl.BlockSpec(memory_space=pltpu.VMEM)
    return pl.pallas_call(
        lambda *refs: inputs_kernel(steps, *refs),
        grid=(model // WIDE,),
        in_specs=[near] * 3,
        out_specs=columns(tokens, WIDE),
        out_shape=shaped((tokens, model), BF16),
        compiler_params=params(16),
        cost_estimate=pl.CostEstimate(
            flops=4 * tokens * model * model, bytes_accessed=6 * model * model, transcendentals=0
        ),
        name="inputs",
    )(grads, direct, weights)


def per_device(
    inputs, gate_in, cotangent, recon_mask, segment_starts, weights, gate_bias, decay_rate
):
    rows, steps, model = inputs.shape
    tokens = rows * steps
    peers, pairs = lax.axis_size("ctx"), lax.axis_size("dp")
    chips = pairs // 2
    summary, grouped, middle, xp = gates(
        inputs, gate_in, cotangent, recon_mask, segment_starts, weights, gate_bias, decay_rate, peers
    )
    slabs = lax.all_to_all(summary, "ctx", 0, 0, tiled=True)
    slabs, xp = lax.optimization_barrier((slabs, xp))
    swap = [(i, i ^ 1) for i in range(pairs)]
    x_other = lax.ppermute(xp, "dp", swap)
    part = model // peers
    gate_grad, grads, sent, direct = gradients(slabs, grouped, middle, xp)
    received = lax.ppermute(sent, "dp", swap)
    x_turned = pl.pallas_call(
        turn_kernel,
        out_shape=shaped((model, 2 * tokens), BF16),
        compiler_params=params(8),
        name="turn",
    )(xp, x_other)
    piece = shaped((2, part, model))
    held, on2, back2 = pl.pallas_call(
        first_weights_kernel,
        out_shape=[shaped((2 * tokens, model), BF16), piece, piece],
        compiler_params=params(12),
        name="first_weights",
    )(x_turned, grads, received)
    on1, back1, on_last, back_last, stay = pl.pallas_call(
        more_weights_kernel,
        out_shape=[piece] * 4 + [shaped((SIDE, part, model))],
        compiler_params=params(12),
        name="more_weights",
    )(x_turned, held)

    def move(value, step, first):
        pairs_of = []
        for i in range(peers * pairs):
            x, y, d = i // pairs // SIDE, i // pairs % SIDE, i % pairs
            if (d % 2 == 0) == first:
                x = (x + step) % SIDE
            else:
                y = (y + step) % SIDE
            pairs_of.append((i, (x * SIDE + y) * pairs + d))
        return lax.ppermute(value, ("ctx", "dp"), pairs_of)

    came_on2, came_back2 = move(on2, 1, True), move(back2, -1, True)
    came_on1, came_back1 = move(on1, 1, True), move(back1, -1, True)
    came_on1, came_back1, direct = lax.optimization_barrier((came_on1, came_back1, direct))
    came_on = move(on_last + came_on2, 1, True)
    came_back = move(back_last + came_back2, -1, True)
    input_grad = input_gradient(grads, direct, weights, steps)
    came_on, came_back, input_grad = lax.optimization_barrier((came_on, came_back, input_grad))
    scale = 1.0 / math.sqrt(rows * pairs * steps * peers)
    near = shaped((part, model))
    quarters = pl.pallas_call(
        fold_kernel,
        out_shape=[near] * SIDE,
        compiler_params=params(8),
        name="fold",
    )(stay, came_back1, came_on, came_on1, came_back)
    others = [move(quarters[d], d, False) for d in (2, 1, 3)]
    by_chip = pl.pallas_call(
        lambda *refs: sum_kernel(scale, *refs),
        out_shape=shaped((chips, part, LANES)),
        compiler_params=params(4),
        name="slab_sum",
    )(quarters[0], *others)
    same_core = [list(range(core, pairs, 2)) for core in range(2)]
    by_chip = lax.all_to_all(
        by_chip, "dp", 0, 0, axis_index_groups=same_core, tiled=True
    )
    total = jnp.sum(by_chip, axis=0)
    return (
        input_grad.reshape(inputs.shape),
        gate_grad.reshape(inputs.shape),
        total,
    )


def solution(mesh):
    return jax.shard_map(
        per_device,
        mesh=mesh,
        in_specs=(
            P("dp", "ctx", None),
            P("dp", "ctx", None),
            P("dp", "ctx", None),
            P("dp", "ctx"),
            P("dp", None),
            P(),
            P(),
            P(),
        ),
        out_specs=(P("dp", "ctx", None), P("dp", "ctx", None), P("ctx", "dp")),
        check_vma=False,
    )
```

```python
import math

import jax
import jax.numpy as jnp
from jax import lax
from jax.experimental import pallas as pl
from jax.experimental.pallas import tpu as pltpu
from jax.sharding import PartitionSpec as P

GROUPS = 8
LANES = 128
BLOCK = 256
F32 = jnp.float32
BF16 = jnp.bfloat16
ROOT = math.sqrt(2.0 / math.pi)
CUBIC = 0.044715
SIDE = 4
WIDE = 512
WIDTH = 512
UNROLL = (16, 16, 16, 16)
PARAMS = (28, 28)
PIECES = (8, 10, 6, 12, 4, 14, 0)


def dot(a, b, dims=((1,), (0,))):
    return lax.dot_general(a, b, (dims, ((), ())), preferred_element_type=F32)


def order(tokens, steps, transpose=False):
    inner = steps // GROUPS
    shift, mask = GROUPS.bit_length() - 1, steps - 1
    rho = lax.broadcasted_iota(jnp.int32, (tokens, tokens), 1 if transpose else 0)
    at = lax.broadcasted_iota(jnp.int32, (tokens, tokens), 0 if transpose else 1)
    place = rho & mask
    source = (rho - place) + (place & (GROUPS - 1)) * inner + (place >> shift)
    return at == source


def wide(value, width):
    return jnp.concatenate([value] * (width // value.shape[1]), axis=1)


def logistic(value):
    return 1.0 / (1.0 + jnp.exp(-value))


def gates_kernel(
    starts, x, gin, cot, mask, w_decay, w_input, bias, rate,
    summary, grouped, middle, xp_out,
    move, move_masked, xb, p1, p2, gins, gos,
):
    tokens, steps = x.shape[0], mask.shape[1]
    rows, inner = tokens // steps, steps // GROUPS
    width = gin.shape[1]
    block = pl.program_id(0)
    me = lax.axis_index("ctx")
    base = me * steps
    lanes = pl.ds(pl.multiple_of(block * width, width), width)
    lanes_input = pl.ds(pl.multiple_of(x.shape[1] + block * width, width), width)

    @pl.when(block == 0)
    def _():
        hit = order(tokens, steps)
        masks = mask[...].astype(F32)
        mask_row = jnp.concatenate([masks[r : r + 1] for r in range(rows)], axis=1)
        move[...] = jnp.where(hit, 1.0, 0.0).astype(BF16)
        move_masked[...] = jnp.where(hit, jnp.broadcast_to(mask_row, hit.shape), 0.0).astype(BF16)
        xp_out[...] = dot(move[...], x[...])
        xb[...] = xp_out[...].astype(BF16)

    p1[...] = dot(xb[...], w_decay[...]) + bias[:, lanes]
    p2[...] = dot(xb[...], w_input[...]) + bias[:, lanes_input]
    gins[...] = dot(move[...], gin[...])
    gos[...] = dot(move_masked[...], cot[...])
    rate8 = jnp.broadcast_to(8.0 * rate[:, lanes], (GROUPS, width))
    spot = lax.broadcasted_iota(jnp.int32, (GROUPS, LANES), 0) * inner + base
    spots = [
        [jnp.broadcast_to(starts[r : r + 1, s : s + 1], spot.shape) for s in range(starts.shape[1])]
        for r in range(rows)
    ]

    def ahead(k, carry):
        new = []
        for r in range(rows):
            h, prod = carry[2 * r], carry[2 * r + 1]
            at = pl.ds(pl.multiple_of(r * steps + k * GROUPS, GROUPS), GROUPS)
            here = spot + k
            reset = here == 0
            for s in range(starts.shape[1]):
                reset = reset | (here == spots[r][s])
            keep = wide(jnp.where(reset, 0.0, 1.0), width)
            gate_decay = logistic(p1[at, :])
            gate_input = logistic(p2[at, :])
            xt = xp_out[at, lanes]
            arg = rate8 * gate_decay
            y = 2.0 * arg
            step = jnp.exp(-arg)
            square = y * (
                1.0 - y * (1 / 2 - y * (1 / 6 - y * (1 / 24 - y * (1 / 120 - y * (1 / 720)))))
            )
            a = keep * step
            c = ((1.0 - keep) + keep * jnp.sqrt(square)) * gate_input
            u = c * xt
            ratio = 0.5 + y * (0.25 + y * (1 / 24 - (y * y) * (1 / 1440)))
            middle[0, at, lanes] = a
            middle[1, at, lanes] = c
            middle[2, at, lanes] = (1.0 - gate_decay) * arg * a
            middle[3, at, lanes] = a * ratio * u
            middle[4, at, lanes] = u * (1.0 - gate_input)
            new += [a * h + u, a * prod]
            g, go = gins[at, :], gos[at, :]
            gsq = g * g
            th = jnp.tanh(ROOT * g * (1.0 + CUBIC * gsq))
            half = 0.5 * (1.0 + th)
            middle[5, at, lanes] = go * (g * half)
            middle[6, at, lanes] = go * (
                half + 0.5 * g * (1.0 - th * th) * (ROOT * (1.0 + (3.0 * CUBIC) * gsq))
            )
        return tuple(new)

    zero = jnp.zeros((GROUPS, width), F32)
    one = jnp.ones((GROUPS, width), F32)
    forward = lax.fori_loop(0, inner, ahead, (zero, one) * rows, unroll=UNROLL[0])

    def back(i, carry):
        k = inner - 1 - i
        new = []
        for r in range(rows):
            at = pl.ds(pl.multiple_of(r * steps + k * GROUPS, GROUPS), GROUPS)
            new.append(middle[0, at, lanes] * (middle[5, at, lanes] + carry[r]))
        return tuple(new)

    backward = lax.fori_loop(0, inner, back, (zero,) * rows, unroll=UNROLL[1])

    for r in range(rows):
        hs, ps, bs = forward[2 * r], forward[2 * r + 1], backward[r]
        grouped[pl.ds((0 * rows + r) * GROUPS, GROUPS), lanes] = ps
        grouped[pl.ds((1 * rows + r) * GROUPS, GROUPS), lanes] = hs
        grouped[pl.ds((2 * rows + r) * GROUPS, GROUPS), lanes] = bs
        qs = ps
        for d in (1, 2, 4):
            hs = ps * pltpu.roll(hs, d, 0) + hs
            ps = ps * pltpu.roll(ps, d, 0)
            bs = qs * pltpu.roll(bs, GROUPS - d, 0) + bs
            qs = qs * pltpu.roll(qs, GROUPS - d, 0)
        for i in range(summary.shape[0]):
            summary[i, r : r + 1, :] = ps[GROUPS - 1 :]
            summary[i, rows + r : rows + r + 1, :] = jnp.where(me < i, hs[GROUPS - 1 :], bs[:1])


def grads_kernel(
    slabs, grouped, middle, xp,
    gate_grad, grads, sent, direct,
    prev, ggs, gds, gis,
):
    count = slabs.shape[0]
    rows = slabs.shape[1] // 2
    tokens, width = gate_grad.shape
    lanes = pl.ds(pl.multiple_of(pl.program_id(0) * width, width), width)
    to_send = pl.ds(pl.multiple_of(pl.program_id(0) * LANES, LANES), LANES)
    steps = tokens // rows
    inner = steps // GROUPS
    me = lax.axis_index("ctx")
    sub = lax.broadcasted_iota(jnp.int32, (GROUPS, width), 0)

    def spread(i, row):
        return jnp.broadcast_to(slabs[i, row : row + 1, lanes], (GROUPS, width))

    enter, enter_back = [], []
    for r in range(rows):
        h = jnp.zeros((GROUPS, width), F32)
        for i in range(count - 1):
            h = jnp.where(i < me, spread(i, r) * h + spread(i, rows + r), h)
        b = jnp.zeros((GROUPS, width), F32)
        for i in range(count - 1, 0, -1):
            b = jnp.where(i > me, spread(i, r) * b + spread(i, rows + r), b)
        ps = grouped[pl.ds((0 * rows + r) * GROUPS, GROUPS), lanes]
        hs = grouped[pl.ds((1 * rows + r) * GROUPS, GROUPS), lanes]
        bs = grouped[pl.ds((2 * rows + r) * GROUPS, GROUPS), lanes]
        hs = jnp.where(sub == 0, ps * h + hs, hs)
        bs = jnp.where(sub == GROUPS - 1, ps * b + bs, bs)
        qs = ps
        for d in (1, 2, 4):
            hs = jnp.where(sub >= d, ps * pltpu.roll(hs, d, 0) + hs, hs)
            ps = jnp.where(sub >= d, ps * pltpu.roll(ps, d, 0), ps)
            bs = jnp.where(sub < GROUPS - d, qs * pltpu.roll(bs, GROUPS - d, 0) + bs, bs)
            qs = jnp.where(sub < GROUPS - d, qs * pltpu.roll(qs, GROUPS - d, 0), qs)
        enter.append(jnp.where(sub == 0, h, pltpu.roll(hs, 1, 0)))
        enter_back.append(jnp.where(sub == GROUPS - 1, b, pltpu.roll(bs, GROUPS - 1, 0)))

    def ahead(k, carry):
        new = []
        for r in range(rows):
            at = pl.ds(pl.multiple_of(r * steps + k * GROUPS, GROUPS), GROUPS)
            prev[at, :] = carry[r]
            h = middle[0, at, lanes] * carry[r] + middle[1, at, lanes] * xp[at, lanes]
            ggs[at, :] = middle[6, at, lanes] * h
            new.append(h)
        return tuple(new)

    lax.fori_loop(0, inner, ahead, tuple(enter), unroll=UNROLL[2])

    def back(i, carry):
        k = inner - 1 - i
        new = []
        for r in range(rows):
            at = pl.ds(pl.multiple_of(r * steps + k * GROUPS, GROUPS), GROUPS)
            adjoint = middle[5, at, lanes] + carry[r]
            new.append(middle[0, at, lanes] * adjoint)
            gds[at, :] = adjoint * middle[2, at, lanes] * (middle[3, at, lanes] - prev[at, :])
            gis[at, :] = adjoint * middle[4, at, lanes]
            direct[at, lanes] = adjoint * middle[1, at, lanes]
        return tuple(new)

    lax.fori_loop(0, inner, back, tuple(enter_back), unroll=UNROLL[3])

    unmove = jnp.where(order(tokens, steps, True), 1.0, 0.0).astype(BF16)
    gate_grad[...] = dot(unmove, ggs[...].astype(BF16)).astype(BF16)
    other = lax.axis_index("dp") % 2 == 0
    for half, value in enumerate((gds, gis)):
        grads[half, :, lanes] = value[...].astype(BF16)
        sent[half, :, to_send] = jnp.where(other, value[:, LANES:], value[:, :LANES])


def turn_kernel(x_own, x_other, out):
    tokens, model = x_own.shape
    part = model // (SIDE * SIDE)
    core = lax.axis_index("dp") % 2
    my_x, my_y = lax.axis_index("ctx") // SIDE, lax.axis_index("ctx") % SIDE
    for s, value in enumerate((x_own, x_other)):
        for bx in range(SIDE):
            turned = value[:, pl.ds(bx * SIDE * part, SIDE * part)].T.astype(BF16)
            for by in range(SIDE):
                dx, dy = (bx - my_x + SIDE) % SIDE, (by - my_y + SIDE) % SIDE
                block = jnp.where(core == 0, dx * SIDE + dy, dy * SIDE + dx)
                to = pl.ds(pl.multiple_of(block * part, part), part)
                out[to, pl.ds(s * tokens, tokens)] = turned[by * part : (by + 1) * part]


def pieces(x_turned, held, outs, starts):
    part = outs[0].shape[1]
    for out, start in zip(outs, starts):
        value = dot(x_turned[pl.ds(start * part, out.shape[0] * part), :], held[...])
        out[...] = value.reshape(out.shape)


def first_weights_kernel(x_turned, grads, received, held, *outs):
    tokens = grads.shape[1]
    core = lax.axis_index("dp") % 2
    parts = grads.shape[2] // (2 * LANES)
    for half in range(2):
        for z in range(parts):
            to = pl.ds((half * parts + z) * LANES, LANES)
            own = jnp.where(
                core == 0,
                grads[half, :, pl.ds(2 * z * LANES, LANES)].astype(F32),
                grads[half, :, pl.ds((2 * z + 1) * LANES, LANES)].astype(F32),
            )
            held[pl.ds(0, tokens), to] = own.astype(BF16)
            held[pl.ds(tokens, tokens), to] = received[
                half, :, pl.ds(z * LANES, LANES)
            ].astype(BF16)
    pieces(x_turned, held, outs, PIECES[:2])


def more_weights_kernel(x_turned, held, *outs):
    pieces(x_turned, held, outs, PIECES[2:])


def fold_kernel(own, low, low_more, high, high_more, *outs):
    for i, out in enumerate(outs):
        first, second = (low, low_more) if i < 2 else (high, high_more)
        out[...] = own[i] + first[i % 2] + second[i % 2]


def inputs_kernel(steps, grads, direct, weights, out):
    model = direct.shape[1]
    tokens, width = out.shape
    at = pl.ds(pl.multiple_of(pl.program_id(0) * width, width), width)
    total = direct[:, at]
    for half in range(2):
        total = total + dot(
            grads[half], weights[at, pl.ds(half * model, model)], ((1,), (1,))
        )
    unmove = jnp.where(order(tokens, steps, True), 1.0, 0.0).astype(BF16)
    out[...] = dot(unmove, total.astype(BF16)).astype(BF16)


def sum_kernel(scale, *refs):
    *parts, out = refs
    for z in range(out.shape[0]):
        at = pl.ds(z * LANES, LANES)
        total = parts[0][:, at]
        for value in parts[1:]:
            total = total + value[:, at]
        out[z] = total * scale


def params(mib):
    return pltpu.CompilerParams(vmem_limit_bytes=mib << 20)


def full(shape):
    return pl.BlockSpec(shape, lambda j: (0,) * len(shape))


def columns(rows, width=BLOCK, first=0):
    return pl.BlockSpec((rows, width), lambda j: (0, j + first))


def far(value):
    return pltpu.with_memory_space_constraint(value, pltpu.HBM)


def shaped(shape, dtype=F32):
    return jax.ShapeDtypeStruct(shape, dtype)


def gates(
    inputs, gate_in, cotangent, recon_mask, segment_starts, weights, gate_bias, decay_rate, peers
):
    rows, steps, model = inputs.shape
    tokens = rows * steps
    blocks = model // WIDTH
    flat = lambda value: value.reshape(tokens, model)
    bias = gate_bias.reshape(1, 2 * model)
    tile = columns(tokens, WIDTH)
    near = pl.BlockSpec(memory_space=pltpu.VMEM)
    return pl.pallas_call(
        gates_kernel,
        grid=(blocks,),
        in_specs=[
            full(segment_starts.shape),
            full((tokens, model)),
            tile,
            tile,
            full((rows, steps)),
            columns(model, WIDTH),
            columns(model, WIDTH, blocks),
            full((1, 2 * model)),
            full((1, model)),
        ],
        out_specs=[pl.BlockSpec((peers, 2 * rows, WIDTH), lambda j: (0, 0, j)), near, near, near],
        out_shape=[
            shaped((peers, 2 * rows, model)),
            pltpu.VMEM((3 * rows * GROUPS, model), F32),
            pltpu.VMEM((7, tokens, model), F32),
            pltpu.VMEM((tokens, model), F32),
        ],
        scratch_shapes=[
            pltpu.VMEM((tokens, tokens), BF16),
            pltpu.VMEM((tokens, tokens), BF16),
            pltpu.VMEM((tokens, model), BF16),
        ]
        + [pltpu.VMEM((tokens, WIDTH), F32)] * 4,
        compiler_params=params(PARAMS[0]),
        name="gates",
    )(
        far(segment_starts), far(flat(inputs)), far(flat(gate_in)), far(flat(cotangent)), far(recon_mask),
        far(weights), far(weights), far(bias), far(decay_rate.reshape(1, model)),
    )


def gradients(slabs, grouped, middle, xp):
    tokens, model = xp.shape
    near = pl.BlockSpec(memory_space=pltpu.VMEM)
    return pl.pallas_call(
        grads_kernel,
        grid=(model // BLOCK,),
        in_specs=[near] * 4,
        out_specs=[columns(tokens), near, near, near],
        out_shape=[
            shaped((tokens, model), BF16),
            pltpu.VMEM((2, tokens, model), BF16),
            pltpu.VMEM((2, tokens, model // 2), F32),
            pltpu.VMEM((tokens, model), F32),
        ],
        scratch_shapes=[pltpu.VMEM((tokens, BLOCK), F32)] * 4,
        compiler_params=params(PARAMS[1]),
        name="grads",
    )(slabs, grouped, middle, xp)


def input_gradient(grads, direct, weights, steps):
    tokens, model = direct.shape
    near = pl.BlockSpec(memory_space=pltpu.VMEM)
    return pl.pallas_call(
        lambda *refs: inputs_kernel(steps, *refs),
        grid=(model // WIDE,),
        in_specs=[near] * 3,
        out_specs=columns(tokens, WIDE),
        out_shape=shaped((tokens, model), BF16),
        compiler_params=params(16),
        cost_estimate=pl.CostEstimate(
            flops=4 * tokens * model * model, bytes_accessed=6 * model * model, transcendentals=0
        ),
        name="inputs",
    )(grads, direct, weights)


def per_device(
    inputs, gate_in, cotangent, recon_mask, segment_starts, weights, gate_bias, decay_rate
):
    rows, steps, model = inputs.shape
    tokens = rows * steps
    peers, pairs = lax.axis_size("ctx"), lax.axis_size("dp")
    chips = pairs // 2
    summary, grouped, middle, xp = gates(
        inputs, gate_in, cotangent, recon_mask, segment_starts, weights, gate_bias, decay_rate, peers
    )
    slabs = lax.all_to_all(summary, "ctx", 0, 0, tiled=True)
    slabs, xp = lax.optimization_barrier((slabs, xp))
    swap = [(i, i ^ 1) for i in range(pairs)]
    x_other = lax.ppermute(xp, "dp", swap)
    part = model // peers
    gate_grad, grads, sent, direct = gradients(slabs, grouped, middle, xp)
    received = lax.ppermute(sent, "dp", swap)
    x_turned = pl.pallas_call(
        turn_kernel,
        out_shape=shaped((model, 2 * tokens), BF16),
        compiler_params=params(8),
        name="turn",
    )(xp, x_other)
    piece = shaped((2, part, model))
    held, on2, back2 = pl.pallas_call(
        first_weights_kernel,
        out_shape=[shaped((2 * tokens, model), BF16), piece, piece],
        compiler_params=params(12),
        name="first_weights",
    )(x_turned, grads, received)
    on1, back1, on_last, back_last, stay = pl.pallas_call(
        more_weights_kernel,
        out_shape=[piece] * 4 + [shaped((SIDE, part, model))],
        compiler_params=params(12),
        name="more_weights",
    )(x_turned, held)

    def move(value, step, first):
        pairs_of = []
        for i in range(peers * pairs):
            x, y, d = i // pairs // SIDE, i // pairs % SIDE, i % pairs
            if (d % 2 == 0) == first:
                x = (x + step) % SIDE
            else:
                y = (y + step) % SIDE
            pairs_of.append((i, (x * SIDE + y) * pairs + d))
        return lax.ppermute(value, ("ctx", "dp"), pairs_of)

    came_on2, came_back2 = move(on2, 1, True), move(back2, -1, True)
    came_on1, came_back1 = move(on1, 1, True), move(back1, -1, True)
    came_on1, came_back1, direct = lax.optimization_barrier((came_on1, came_back1, direct))
    came_on = move(on_last + came_on2, 1, True)
    came_back = move(back_last + came_back2, -1, True)
    input_grad = input_gradient(grads, direct, weights, steps)
    came_on, came_back, input_grad = lax.optimization_barrier((came_on, came_back, input_grad))
    scale = 1.0 / math.sqrt(rows * pairs * steps * peers)
    near = shaped((part, model))
    quarters = pl.pallas_call(
        fold_kernel,
        out_shape=[near] * SIDE,
        compiler_params=params(8),
        name="fold",
    )(stay, came_back1, came_on, came_on1, came_back)
    others = [move(quarters[d], d, False) for d in (2, 1, 3)]
    by_chip = pl.pallas_call(
        lambda *refs: sum_kernel(scale, *refs),
        out_shape=shaped((chips, part, LANES)),
        compiler_params=params(4),
        name="slab_sum",
    )(quarters[0], *others)
    same_core = [list(range(core, pairs, 2)) for core in range(2)]
    by_chip = lax.all_to_all(
        by_chip, "dp", 0, 0, axis_index_groups=same_core, tiled=True
    )
    total = jnp.sum(by_chip, axis=0)
    return (
        input_grad.reshape(inputs.shape),
        gate_grad.reshape(inputs.shape),
        total,
    )


def solution(mesh):
    return jax.shard_map(
        per_device,
        mesh=mesh,
        in_specs=(
            P("dp", "ctx", None),
            P("dp", "ctx", None),
            P("dp", "ctx", None),
            P("dp", "ctx"),
            P("dp", None),
            P(),
            P(),
            P(),
        ),
        out_specs=(P("dp", "ctx", None), P("dp", "ctx", None), P("ctx", "dp")),
        check_vma=False,
    )
```

```python
import math

import jax
import jax.numpy as jnp
from jax import lax
from jax.experimental import pallas as pl
from jax.experimental.pallas import tpu as pltpu
from jax.sharding import PartitionSpec as P

GROUPS = 8
LANES = 128
BLOCK = 256
F32 = jnp.float32
BF16 = jnp.bfloat16
ROOT = math.sqrt(2.0 / math.pi)
CUBIC = 0.044715
SIDE = 4
WIDE = 512
WIDTH = 512
SPAN = 512
UNROLL = (16, 16, 16, 16)
PARAMS = (28, 28)
PIECES = (8, 10, 6, 12, 4, 14, 0)


def dot(a, b, dims=((1,), (0,))):
    return lax.dot_general(a, b, (dims, ((), ())), preferred_element_type=F32)


def order(tokens, steps, transpose=False):
    inner = steps // GROUPS
    shift, mask = GROUPS.bit_length() - 1, steps - 1
    rho = lax.broadcasted_iota(jnp.int32, (tokens, tokens), 1 if transpose else 0)
    at = lax.broadcasted_iota(jnp.int32, (tokens, tokens), 0 if transpose else 1)
    place = rho & mask
    source = (rho - place) + (place & (GROUPS - 1)) * inner + (place >> shift)
    return at == source


def wide(value, width):
    return jnp.concatenate([value] * (width // value.shape[1]), axis=1)


def logistic(value):
    return 1.0 / (1.0 + jnp.exp(-value))


def gates_kernel(
    starts, x, gin, cot, mask, w_decay, w_input, bias, rate,
    summary, grouped, middle, xp_out,
    move, move_masked, xb, p1, p2, gins, gos,
):
    tokens, steps = x.shape[0], mask.shape[1]
    rows, inner = tokens // steps, steps // GROUPS
    width = gin.shape[1]
    block = pl.program_id(0)
    me = lax.axis_index("ctx")
    base = me * steps
    lanes = pl.ds(pl.multiple_of(block * width, width), width)
    lanes_input = pl.ds(pl.multiple_of(x.shape[1] + block * width, width), width)

    @pl.when(block == 0)
    def _():
        hit = order(tokens, steps)
        masks = mask[...].astype(F32)
        mask_row = jnp.concatenate([masks[r : r + 1] for r in range(rows)], axis=1)
        move[...] = jnp.where(hit, 1.0, 0.0).astype(BF16)
        move_masked[...] = jnp.where(hit, jnp.broadcast_to(mask_row, hit.shape), 0.0).astype(BF16)
        xp_out[...] = dot(move[...], x[...])
        xb[...] = xp_out[...].astype(BF16)

    p1[...] = dot(xb[...], w_decay[...]) + bias[:, lanes]
    p2[...] = dot(xb[...], w_input[...]) + bias[:, lanes_input]
    gins[...] = dot(move[...], gin[...])
    gos[...] = dot(move_masked[...], cot[...])
    rate8 = jnp.broadcast_to(8.0 * rate[:, lanes], (GROUPS, width))
    spot = lax.broadcasted_iota(jnp.int32, (GROUPS, LANES), 0) * inner + base
    spots = [
        [jnp.broadcast_to(starts[r : r + 1, s : s + 1], spot.shape) for s in range(starts.shape[1])]
        for r in range(rows)
    ]

    def ahead(k, carry):
        new = []
        for r in range(rows):
            h, prod = carry[2 * r], carry[2 * r + 1]
            at = pl.ds(pl.multiple_of(r * steps + k * GROUPS, GROUPS), GROUPS)
            here = spot + k
            reset = here == 0
            for s in range(starts.shape[1]):
                reset = reset | (here == spots[r][s])
            keep = wide(jnp.where(reset, 0.0, 1.0), width)
            gate_decay = logistic(p1[at, :])
            gate_input = logistic(p2[at, :])
            xt = xp_out[at, lanes]
            arg = rate8 * gate_decay
            y = 2.0 * arg
            step = jnp.exp(-arg)
            square = y * (
                1.0 - y * (1 / 2 - y * (1 / 6 - y * (1 / 24 - y * (1 / 120 - y * (1 / 720)))))
            )
            a = keep * step
            c = ((1.0 - keep) + keep * jnp.sqrt(square)) * gate_input
            u = c * xt
            ratio = 0.5 + y * (0.25 + y * (1 / 24 - (y * y) * (1 / 1440)))
            middle[0, at, lanes] = a
            middle[1, at, lanes] = c
            middle[2, at, lanes] = (1.0 - gate_decay) * arg * a
            middle[3, at, lanes] = a * ratio * u
            middle[4, at, lanes] = u * (1.0 - gate_input)
            new += [a * h + u, a * prod]
            g, go = gins[at, :], gos[at, :]
            gsq = g * g
            th = jnp.tanh(ROOT * g * (1.0 + CUBIC * gsq))
            half = 0.5 * (1.0 + th)
            middle[5, at, lanes] = go * (g * half)
            middle[6, at, lanes] = go * (
                half + 0.5 * g * (1.0 - th * th) * (ROOT * (1.0 + (3.0 * CUBIC) * gsq))
            )
        return tuple(new)

    zero = jnp.zeros((GROUPS, width), F32)
    one = jnp.ones((GROUPS, width), F32)
    forward = lax.fori_loop(0, inner, ahead, (zero, one) * rows, unroll=UNROLL[0])

    def back(i, carry):
        k = inner - 1 - i
        new = []
        for r in range(rows):
            at = pl.ds(pl.multiple_of(r * steps + k * GROUPS, GROUPS), GROUPS)
            new.append(middle[0, at, lanes] * (middle[5, at, lanes] + carry[r]))
        return tuple(new)

    backward = lax.fori_loop(0, inner, back, (zero,) * rows, unroll=UNROLL[1])

    for r in range(rows):
        hs, ps, bs = forward[2 * r], forward[2 * r + 1], backward[r]
        grouped[pl.ds((0 * rows + r) * GROUPS, GROUPS), lanes] = ps
        grouped[pl.ds((1 * rows + r) * GROUPS, GROUPS), lanes] = hs
        grouped[pl.ds((2 * rows + r) * GROUPS, GROUPS), lanes] = bs
        qs = ps
        for d in (1, 2, 4):
            hs = ps * pltpu.roll(hs, d, 0) + hs
            ps = ps * pltpu.roll(ps, d, 0)
            bs = qs * pltpu.roll(bs, GROUPS - d, 0) + bs
            qs = qs * pltpu.roll(qs, GROUPS - d, 0)
        for i in range(summary.shape[0]):
            summary[i, r : r + 1, :] = ps[GROUPS - 1 :]
            summary[i, rows + r : rows + r + 1, :] = jnp.where(me < i, hs[GROUPS - 1 :], bs[:1])


def grads_kernel(
    slabs, grouped, middle, xp,
    gate_grad, grads, sent, direct,
    prev, ggs, gds, gis,
):
    count = slabs.shape[0]
    rows = slabs.shape[1] // 2
    tokens, width = gate_grad.shape
    lanes = pl.ds(pl.multiple_of(pl.program_id(0) * width, width), width)
    steps = tokens // rows
    inner = steps // GROUPS
    me = lax.axis_index("ctx")
    sub = lax.broadcasted_iota(jnp.int32, (GROUPS, width), 0)

    def spread(i, row):
        return jnp.broadcast_to(slabs[i, row : row + 1, lanes], (GROUPS, width))

    enter, enter_back = [], []
    for r in range(rows):
        h = jnp.zeros((GROUPS, width), F32)
        for i in range(count - 1):
            h = jnp.where(i < me, spread(i, r) * h + spread(i, rows + r), h)
        b = jnp.zeros((GROUPS, width), F32)
        for i in range(count - 1, 0, -1):
            b = jnp.where(i > me, spread(i, r) * b + spread(i, rows + r), b)
        ps = grouped[pl.ds((0 * rows + r) * GROUPS, GROUPS), lanes]
        hs = grouped[pl.ds((1 * rows + r) * GROUPS, GROUPS), lanes]
        bs = grouped[pl.ds((2 * rows + r) * GROUPS, GROUPS), lanes]
        hs = jnp.where(sub == 0, ps * h + hs, hs)
        bs = jnp.where(sub == GROUPS - 1, ps * b + bs, bs)
        qs = ps
        for d in (1, 2, 4):
            hs = jnp.where(sub >= d, ps * pltpu.roll(hs, d, 0) + hs, hs)
            ps = jnp.where(sub >= d, ps * pltpu.roll(ps, d, 0), ps)
            bs = jnp.where(sub < GROUPS - d, qs * pltpu.roll(bs, GROUPS - d, 0) + bs, bs)
            qs = jnp.where(sub < GROUPS - d, qs * pltpu.roll(qs, GROUPS - d, 0), qs)
        enter.append(jnp.where(sub == 0, h, pltpu.roll(hs, 1, 0)))
        enter_back.append(jnp.where(sub == GROUPS - 1, b, pltpu.roll(bs, GROUPS - 1, 0)))

    def ahead(k, carry):
        new = []
        for r in range(rows):
            at = pl.ds(pl.multiple_of(r * steps + k * GROUPS, GROUPS), GROUPS)
            prev[at, :] = carry[r]
            h = middle[0, at, lanes] * carry[r] + middle[1, at, lanes] * xp[at, lanes]
            ggs[at, :] = middle[6, at, lanes] * h
            new.append(h)
        return tuple(new)

    lax.fori_loop(0, inner, ahead, tuple(enter), unroll=UNROLL[2])

    def back(i, carry):
        k = inner - 1 - i
        new = []
        for r in range(rows):
            at = pl.ds(pl.multiple_of(r * steps + k * GROUPS, GROUPS), GROUPS)
            adjoint = middle[5, at, lanes] + carry[r]
            new.append(middle[0, at, lanes] * adjoint)
            gds[at, :] = adjoint * middle[2, at, lanes] * (middle[3, at, lanes] - prev[at, :])
            gis[at, :] = adjoint * middle[4, at, lanes]
            direct[at, lanes] = adjoint * middle[1, at, lanes]
        return tuple(new)

    lax.fori_loop(0, inner, back, tuple(enter_back), unroll=UNROLL[3])

    unmove = jnp.where(order(tokens, steps, True), 1.0, 0.0).astype(BF16)
    gate_grad[...] = dot(unmove, ggs[...].astype(BF16)).astype(BF16)
    other = lax.axis_index("dp") % 2 == 0
    for half, value in enumerate((gds, gis)):
        grads[half, :, lanes] = value[...].astype(BF16)
        for i in range(width // (2 * LANES)):
            spot = pl.program_id(0) * (width // 2) + i * LANES
            to_send = pl.ds(pl.multiple_of(spot, LANES), LANES)
            low, high = pl.ds(2 * i * LANES, LANES), pl.ds((2 * i + 1) * LANES, LANES)
            sent[half, :, to_send] = jnp.where(other, value[:, high], value[:, low])


def turn_kernel(x_own, x_other, out):
    tokens, model = x_own.shape
    part = model // (SIDE * SIDE)
    core = lax.axis_index("dp") % 2
    my_x, my_y = lax.axis_index("ctx") // SIDE, lax.axis_index("ctx") % SIDE
    for s, value in enumerate((x_own, x_other)):
        for bx in range(SIDE):
            turned = value[:, pl.ds(bx * SIDE * part, SIDE * part)].T.astype(BF16)
            for by in range(SIDE):
                dx, dy = (bx - my_x + SIDE) % SIDE, (by - my_y + SIDE) % SIDE
                block = jnp.where(core == 0, dx * SIDE + dy, dy * SIDE + dx)
                to = pl.ds(pl.multiple_of(block * part, part), part)
                out[to, pl.ds(s * tokens, tokens)] = turned[by * part : (by + 1) * part]


def pieces(x_turned, held, outs, starts):
    part = outs[0].shape[1]
    for out, start in zip(outs, starts):
        value = dot(x_turned[pl.ds(start * part, out.shape[0] * part), :], held[...])
        out[...] = value.reshape(out.shape)


def first_weights_kernel(x_turned, grads, received, held, *outs):
    tokens = grads.shape[1]
    core = lax.axis_index("dp") % 2
    parts = grads.shape[2] // (2 * LANES)
    for half in range(2):
        for z in range(parts):
            to = pl.ds((half * parts + z) * LANES, LANES)
            own = jnp.where(
                core == 0,
                grads[half, :, pl.ds(2 * z * LANES, LANES)].astype(F32),
                grads[half, :, pl.ds((2 * z + 1) * LANES, LANES)].astype(F32),
            )
            held[pl.ds(0, tokens), to] = own.astype(BF16)
            held[pl.ds(tokens, tokens), to] = received[
                half, :, pl.ds(z * LANES, LANES)
            ].astype(BF16)
    pieces(x_turned, held, outs, PIECES[:2])


def more_weights_kernel(x_turned, held, *outs):
    pieces(x_turned, held, outs, PIECES[2:])


def fold_kernel(own, low, low_more, high, high_more, *outs):
    for i, out in enumerate(outs):
        first, second = (low, low_more) if i < 2 else (high, high_more)
        out[...] = own[i] + first[i % 2] + second[i % 2]


def inputs_kernel(steps, grads, direct, weights, out):
    model = direct.shape[1]
    tokens, width = out.shape
    at = pl.ds(pl.multiple_of(pl.program_id(0) * width, width), width)
    total = direct[:, at]
    for half in range(2):
        total = total + dot(
            grads[half], weights[at, pl.ds(half * model, model)], ((1,), (1,))
        )
    unmove = jnp.where(order(tokens, steps, True), 1.0, 0.0).astype(BF16)
    out[...] = dot(unmove, total.astype(BF16)).astype(BF16)


def sum_kernel(scale, *refs):
    *parts, out = refs
    for z in range(out.shape[0]):
        at = pl.ds(z * LANES, LANES)
        total = parts[0][:, at]
        for value in parts[1:]:
            total = total + value[:, at]
        out[z] = total * scale


def params(mib):
    return pltpu.CompilerParams(vmem_limit_bytes=mib << 20)


def full(shape):
    return pl.BlockSpec(shape, lambda j: (0,) * len(shape))


def columns(rows, width=BLOCK, first=0):
    return pl.BlockSpec((rows, width), lambda j: (0, j + first))


def far(value):
    return pltpu.with_memory_space_constraint(value, pltpu.HBM)


def shaped(shape, dtype=F32):
    return jax.ShapeDtypeStruct(shape, dtype)


def gates(
    inputs, gate_in, cotangent, recon_mask, segment_starts, weights, gate_bias, decay_rate, peers
):
    rows, steps, model = inputs.shape
    tokens = rows * steps
    blocks = model // WIDTH
    flat = lambda value: value.reshape(tokens, model)
    bias = gate_bias.reshape(1, 2 * model)
    tile = columns(tokens, WIDTH)
    near = pl.BlockSpec(memory_space=pltpu.VMEM)
    return pl.pallas_call(
        gates_kernel,
        grid=(blocks,),
        in_specs=[
            full(segment_starts.shape),
            full((tokens, model)),
            tile,
            tile,
            full((rows, steps)),
            columns(model, WIDTH),
            columns(model, WIDTH, blocks),
            full((1, 2 * model)),
            full((1, model)),
        ],
        out_specs=[pl.BlockSpec((peers, 2 * rows, WIDTH), lambda j: (0, 0, j)), near, near, near],
        out_shape=[
            shaped((peers, 2 * rows, model)),
            pltpu.VMEM((3 * rows * GROUPS, model), F32),
            pltpu.VMEM((7, tokens, model), F32),
            pltpu.VMEM((tokens, model), F32),
        ],
        scratch_shapes=[
            pltpu.VMEM((tokens, tokens), BF16),
            pltpu.VMEM((tokens, tokens), BF16),
            pltpu.VMEM((tokens, model), BF16),
        ]
        + [pltpu.VMEM((tokens, WIDTH), F32)] * 4,
        compiler_params=params(PARAMS[0]),
        name="gates",
    )(
        far(segment_starts), far(flat(inputs)), far(flat(gate_in)), far(flat(cotangent)), far(recon_mask),
        far(weights), far(weights), far(bias), far(decay_rate.reshape(1, model)),
    )


def gradients(slabs, grouped, middle, xp):
    tokens, model = xp.shape
    near = pl.BlockSpec(memory_space=pltpu.VMEM)
    return pl.pallas_call(
        grads_kernel,
        grid=(model // SPAN,),
        in_specs=[near] * 4,
        out_specs=[columns(tokens, SPAN), near, near, near],
        out_shape=[
            shaped((tokens, model), BF16),
            pltpu.VMEM((2, tokens, model), BF16),
            pltpu.VMEM((2, tokens, model // 2), F32),
            pltpu.VMEM((tokens, model), F32),
        ],
        scratch_shapes=[pltpu.VMEM((tokens, SPAN), F32)] * 4,
        compiler_params=params(PARAMS[1]),
        name="grads",
    )(slabs, grouped, middle, xp)


def input_gradient(grads, direct, weights, steps):
    tokens, model = direct.shape
    near = pl.BlockSpec(memory_space=pltpu.VMEM)
    return pl.pallas_call(
        lambda *refs: inputs_kernel(steps, *refs),
        grid=(model // WIDE,),
        in_specs=[near] * 3,
        out_specs=columns(tokens, WIDE),
        out_shape=shaped((tokens, model), BF16),
        compiler_params=params(16),
        cost_estimate=pl.CostEstimate(
            flops=4 * tokens * model * model, bytes_accessed=6 * model * model, transcendentals=0
        ),
        name="inputs",
    )(grads, direct, weights)


def per_device(
    inputs, gate_in, cotangent, recon_mask, segment_starts, weights, gate_bias, decay_rate
):
    rows, steps, model = inputs.shape
    tokens = rows * steps
    peers, pairs = lax.axis_size("ctx"), lax.axis_size("dp")
    chips = pairs // 2
    summary, grouped, middle, xp = gates(
        inputs, gate_in, cotangent, recon_mask, segment_starts, weights, gate_bias, decay_rate, peers
    )
    slabs = lax.all_to_all(summary, "ctx", 0, 0, tiled=True)
    slabs, xp = lax.optimization_barrier((slabs, xp))
    swap = [(i, i ^ 1) for i in range(pairs)]
    x_other = lax.ppermute(xp, "dp", swap)
    part = model // peers
    gate_grad, grads, sent, direct = gradients(slabs, grouped, middle, xp)
    received = lax.ppermute(sent, "dp", swap)
    x_turned = pl.pallas_call(
        turn_kernel,
        out_shape=shaped((model, 2 * tokens), BF16),
        compiler_params=params(8),
        name="turn",
    )(xp, x_other)
    piece = shaped((2, part, model))
    held, on2, back2 = pl.pallas_call(
        first_weights_kernel,
        out_shape=[shaped((2 * tokens, model), BF16), piece, piece],
        compiler_params=params(12),
        name="first_weights",
    )(x_turned, grads, received)
    on1, back1, on_last, back_last, stay = pl.pallas_call(
        more_weights_kernel,
        out_shape=[piece] * 4 + [shaped((SIDE, part, model))],
        compiler_params=params(12),
        name="more_weights",
    )(x_turned, held)

    def move(value, step, first):
        pairs_of = []
        for i in range(peers * pairs):
            x, y, d = i // pairs // SIDE, i // pairs % SIDE, i % pairs
            if (d % 2 == 0) == first:
                x = (x + step) % SIDE
            else:
                y = (y + step) % SIDE
            pairs_of.append((i, (x * SIDE + y) * pairs + d))
        return lax.ppermute(value, ("ctx", "dp"), pairs_of)

    came_on2, came_back2 = move(on2, 1, True), move(back2, -1, True)
    came_on1, came_back1 = move(on1, 1, True), move(back1, -1, True)
    came_on1, came_back1, direct = lax.optimization_barrier((came_on1, came_back1, direct))
    came_on = move(on_last + came_on2, 1, True)
    came_back = move(back_last + came_back2, -1, True)
    input_grad = input_gradient(grads, direct, weights, steps)
    came_on, came_back, input_grad = lax.optimization_barrier((came_on, came_back, input_grad))
    scale = 1.0 / math.sqrt(rows * pairs * steps * peers)
    near = shaped((part, model))
    quarters = pl.pallas_call(
        fold_kernel,
        out_shape=[near] * SIDE,
        compiler_params=params(8),
        name="fold",
    )(stay, came_back1, came_on, came_on1, came_back)
    others = [move(quarters[d], d, False) for d in (2, 1, 3)]
    by_chip = pl.pallas_call(
        lambda *refs: sum_kernel(scale, *refs),
        out_shape=shaped((chips, part, LANES)),
        compiler_params=params(4),
        name="slab_sum",
    )(quarters[0], *others)
    same_core = [list(range(core, pairs, 2)) for core in range(2)]
    by_chip = lax.all_to_all(
        by_chip, "dp", 0, 0, axis_index_groups=same_core, tiled=True
    )
    total = jnp.sum(by_chip, axis=0)
    return (
        input_grad.reshape(inputs.shape),
        gate_grad.reshape(inputs.shape),
        total,
    )


def solution(mesh):
    return jax.shard_map(
        per_device,
        mesh=mesh,
        in_specs=(
            P("dp", "ctx", None),
            P("dp", "ctx", None),
            P("dp", "ctx", None),
            P("dp", "ctx"),
            P("dp", None),
            P(),
            P(),
            P(),
        ),
        out_specs=(P("dp", "ctx", None), P("dp", "ctx", None), P("ctx", "dp")),
        check_vma=False,
    )
```

```python
import math

import jax
import jax.numpy as jnp
from jax import lax
from jax.experimental import pallas as pl
from jax.experimental.pallas import tpu as pltpu
from jax.sharding import PartitionSpec as P

GROUPS = 8
LANES = 128
BLOCK = 256
F32 = jnp.float32
BF16 = jnp.bfloat16
ROOT = math.sqrt(2.0 / math.pi)
CUBIC = 0.044715
SIDE = 4
WIDE = 512
WIDTH = 512
SPAN = 512
UNROLL = (16, 16, 16, 16)
PARAMS = (28, 28)
PIECES = (8, 10, 6, 12, 4, 14, 0)


def dot(a, b, dims=((1,), (0,))):
    return lax.dot_general(a, b, (dims, ((), ())), preferred_element_type=F32)


def order(tokens, steps, transpose=False):
    inner = steps // GROUPS
    shift, mask = GROUPS.bit_length() - 1, steps - 1
    rho = lax.broadcasted_iota(jnp.int32, (tokens, tokens), 1 if transpose else 0)
    at = lax.broadcasted_iota(jnp.int32, (tokens, tokens), 0 if transpose else 1)
    place = rho & mask
    source = (rho - place) + (place & (GROUPS - 1)) * inner + (place >> shift)
    return at == source


def wide(value, width):
    return jnp.concatenate([value] * (width // value.shape[1]), axis=1)


def logistic(value):
    return 1.0 / (1.0 + jnp.exp(-value))


def gates_kernel(
    starts, x, gin, cot, mask, w_decay, w_input, bias, rate,
    summary, grouped, middle, xp_out,
    move, move_masked, xb, p1, p2, gins, gos,
):
    tokens, steps = x.shape[0], mask.shape[1]
    rows, inner = tokens // steps, steps // GROUPS
    width = gin.shape[1]
    block = pl.program_id(0)
    me = lax.axis_index("ctx")
    base = me * steps
    lanes = pl.ds(pl.multiple_of(block * width, width), width)
    lanes_input = pl.ds(pl.multiple_of(x.shape[1] + block * width, width), width)

    @pl.when(block == 0)
    def _():
        hit = order(tokens, steps)
        masks = mask[...].astype(F32)
        mask_row = jnp.concatenate([masks[r : r + 1] for r in range(rows)], axis=1)
        move[...] = jnp.where(hit, 1.0, 0.0).astype(BF16)
        move_masked[...] = jnp.where(hit, jnp.broadcast_to(mask_row, hit.shape), 0.0).astype(BF16)
        xp_out[...] = dot(move[...], x[...])
        xb[...] = xp_out[...].astype(BF16)

    p1[...] = dot(xb[...], w_decay[...]) + bias[:, lanes]
    p2[...] = dot(xb[...], w_input[...]) + bias[:, lanes_input]
    gins[...] = dot(move[...], gin[...])
    gos[...] = dot(move_masked[...], cot[...])
    rate8 = jnp.broadcast_to(8.0 * rate[:, lanes], (GROUPS, width))
    spot = lax.broadcasted_iota(jnp.int32, (GROUPS, LANES), 0) * inner + base
    spots = [
        [jnp.broadcast_to(starts[r : r + 1, s : s + 1], spot.shape) for s in range(starts.shape[1])]
        for r in range(rows)
    ]

    def ahead(k, carry):
        new = []
        for r in range(rows):
            h, prod = carry[2 * r], carry[2 * r + 1]
            at = pl.ds(pl.multiple_of(r * steps + k * GROUPS, GROUPS), GROUPS)
            here = spot + k
            reset = here == 0
            for s in range(starts.shape[1]):
                reset = reset | (here == spots[r][s])
            keep = wide(jnp.where(reset, 0.0, 1.0), width)
            gate_decay = logistic(p1[at, :])
            gate_input = logistic(p2[at, :])
            xt = xp_out[at, lanes]
            arg = rate8 * gate_decay
            y = 2.0 * arg
            step = jnp.exp(-arg)
            square = y * (
                1.0 - y * (1 / 2 - y * (1 / 6 - y * (1 / 24 - y * (1 / 120 - y * (1 / 720)))))
            )
            a = keep * step
            c = ((1.0 - keep) + keep * jnp.sqrt(square)) * gate_input
            u = c * xt
            ratio = 0.5 + y * (0.25 + y * (1 / 24 - (y * y) * (1 / 1440)))
            middle[0, at, lanes] = a
            middle[1, at, lanes] = c
            middle[2, at, lanes] = (1.0 - gate_decay) * arg * a
            middle[3, at, lanes] = a * ratio * u
            middle[4, at, lanes] = u * (1.0 - gate_input)
            new += [a * h + u, a * prod]
            g, go = gins[at, :], gos[at, :]
            gsq = g * g
            th = jnp.tanh(ROOT * g * (1.0 + CUBIC * gsq))
            half = 0.5 * (1.0 + th)
            middle[5, at, lanes] = go * (g * half)
            middle[6, at, lanes] = go * (
                half + 0.5 * g * (1.0 - th * th) * (ROOT * (1.0 + (3.0 * CUBIC) * gsq))
            )
        return tuple(new)

    zero = jnp.zeros((GROUPS, width), F32)
    one = jnp.ones((GROUPS, width), F32)
    forward = lax.fori_loop(0, inner, ahead, (zero, one) * rows, unroll=UNROLL[0])

    def back(i, carry):
        k = inner - 1 - i
        new = []
        for r in range(rows):
            at = pl.ds(pl.multiple_of(r * steps + k * GROUPS, GROUPS), GROUPS)
            new.append(middle[0, at, lanes] * (middle[5, at, lanes] + carry[r]))
        return tuple(new)

    backward = lax.fori_loop(0, inner, back, (zero,) * rows, unroll=UNROLL[1])

    for r in range(rows):
        hs, ps, bs = forward[2 * r], forward[2 * r + 1], backward[r]
        grouped[pl.ds((0 * rows + r) * GROUPS, GROUPS), lanes] = ps
        grouped[pl.ds((1 * rows + r) * GROUPS, GROUPS), lanes] = hs
        grouped[pl.ds((2 * rows + r) * GROUPS, GROUPS), lanes] = bs
        qs = ps
        for d in (1, 2, 4):
            hs = ps * pltpu.roll(hs, d, 0) + hs
            ps = ps * pltpu.roll(ps, d, 0)
            bs = qs * pltpu.roll(bs, GROUPS - d, 0) + bs
            qs = qs * pltpu.roll(qs, GROUPS - d, 0)
        for i in range(summary.shape[0]):
            summary[i, r : r + 1, :] = ps[GROUPS - 1 :]
            summary[i, rows + r : rows + r + 1, :] = jnp.where(me < i, hs[GROUPS - 1 :], bs[:1])


def grads_kernel(
    slabs, grouped, middle, xp,
    gate_grad, grads, sent, direct,
    prev, ggs, gds, gis,
):
    count = slabs.shape[0]
    rows = slabs.shape[1] // 2
    tokens, width = gate_grad.shape
    lanes = pl.ds(pl.multiple_of(pl.program_id(0) * width, width), width)
    steps = tokens // rows
    inner = steps // GROUPS
    me = lax.axis_index("ctx")
    sub = lax.broadcasted_iota(jnp.int32, (GROUPS, width), 0)

    def spread(i, row):
        return jnp.broadcast_to(slabs[i, row : row + 1, lanes], (GROUPS, width))

    enter, enter_back = [], []
    for r in range(rows):
        h = jnp.zeros((GROUPS, width), F32)
        for i in range(count - 1):
            h = jnp.where(i < me, spread(i, r) * h + spread(i, rows + r), h)
        b = jnp.zeros((GROUPS, width), F32)
        for i in range(count - 1, 0, -1):
            b = jnp.where(i > me, spread(i, r) * b + spread(i, rows + r), b)
        ps = grouped[pl.ds((0 * rows + r) * GROUPS, GROUPS), lanes]
        hs = grouped[pl.ds((1 * rows + r) * GROUPS, GROUPS), lanes]
        bs = grouped[pl.ds((2 * rows + r) * GROUPS, GROUPS), lanes]
        hs = jnp.where(sub == 0, ps * h + hs, hs)
        bs = jnp.where(sub == GROUPS - 1, ps * b + bs, bs)
        qs = ps
        for d in (1, 2, 4):
            hs = jnp.where(sub >= d, ps * pltpu.roll(hs, d, 0) + hs, hs)
            ps = jnp.where(sub >= d, ps * pltpu.roll(ps, d, 0), ps)
            bs = jnp.where(sub < GROUPS - d, qs * pltpu.roll(bs, GROUPS - d, 0) + bs, bs)
            qs = jnp.where(sub < GROUPS - d, qs * pltpu.roll(qs, GROUPS - d, 0), qs)
        enter.append(jnp.where(sub == 0, h, pltpu.roll(hs, 1, 0)))
        enter_back.append(jnp.where(sub == GROUPS - 1, b, pltpu.roll(bs, GROUPS - 1, 0)))

    def ahead(k, carry):
        new = []
        for r in range(rows):
            at = pl.ds(pl.multiple_of(r * steps + k * GROUPS, GROUPS), GROUPS)
            prev[at, :] = carry[r]
            h = middle[0, at, lanes] * carry[r] + middle[1, at, lanes] * xp[at, lanes]
            ggs[at, :] = middle[6, at, lanes] * h
            new.append(h)
        return tuple(new)

    lax.fori_loop(0, inner, ahead, tuple(enter), unroll=UNROLL[2])

    def back(i, carry):
        k = inner - 1 - i
        new = []
        for r in range(rows):
            at = pl.ds(pl.multiple_of(r * steps + k * GROUPS, GROUPS), GROUPS)
            adjoint = middle[5, at, lanes] + carry[r]
            new.append(middle[0, at, lanes] * adjoint)
            gds[at, :] = adjoint * middle[2, at, lanes] * (middle[3, at, lanes] - prev[at, :])
            gis[at, :] = adjoint * middle[4, at, lanes]
            direct[at, lanes] = adjoint * middle[1, at, lanes]
        return tuple(new)

    lax.fori_loop(0, inner, back, tuple(enter_back), unroll=UNROLL[3])

    unmove = jnp.where(order(tokens, steps, True), 1.0, 0.0).astype(BF16)
    gate_grad[...] = dot(unmove, ggs[...].astype(BF16)).astype(BF16)
    other = lax.axis_index("dp") % 2 == 0
    for half, value in enumerate((gds, gis)):
        grads[half, :, lanes] = value[...].astype(BF16)
        for i in range(width // (2 * LANES)):
            spot = pl.program_id(0) * (width // 2) + i * LANES
            to_send = pl.ds(pl.multiple_of(spot, LANES), LANES)
            low, high = pl.ds(2 * i * LANES, LANES), pl.ds((2 * i + 1) * LANES, LANES)
            sent[half, :, to_send] = jnp.where(other, value[:, high], value[:, low])


def turn_kernel(x_own, x_other, grads, out, held):
    tokens, model = x_own.shape
    part = model // (SIDE * SIDE)
    core = lax.axis_index("dp") % 2
    my_x, my_y = lax.axis_index("ctx") // SIDE, lax.axis_index("ctx") % SIDE
    for s, value in enumerate((x_own, x_other)):
        for bx in range(SIDE):
            turned = value[:, pl.ds(bx * SIDE * part, SIDE * part)].T.astype(BF16)
            for by in range(SIDE):
                dx, dy = (bx - my_x + SIDE) % SIDE, (by - my_y + SIDE) % SIDE
                block = jnp.where(core == 0, dx * SIDE + dy, dy * SIDE + dx)
                to = pl.ds(pl.multiple_of(block * part, part), part)
                out[to, pl.ds(s * tokens, tokens)] = turned[by * part : (by + 1) * part]
    parts = grads.shape[2] // (2 * LANES)
    for half in range(2):
        for z in range(parts):
            to = pl.ds((half * parts + z) * LANES, LANES)
            own = jnp.where(
                core == 0,
                grads[half, :, pl.ds(2 * z * LANES, LANES)].astype(F32),
                grads[half, :, pl.ds((2 * z + 1) * LANES, LANES)].astype(F32),
            )
            held[pl.ds(0, tokens), to] = own.astype(BF16)


def pieces(x_turned, held, outs, starts):
    part = outs[0].shape[1]
    for out, start in zip(outs, starts):
        value = dot(x_turned[pl.ds(start * part, out.shape[0] * part), :], held[...])
        out[...] = value.reshape(out.shape)


def first_weights_kernel(x_turned, received, held_own, held, *outs):
    tokens = received.shape[1]
    parts = received.shape[2] // LANES
    for half in range(2):
        for z in range(parts):
            to = pl.ds((half * parts + z) * LANES, LANES)
            held[pl.ds(tokens, tokens), to] = received[
                half, :, pl.ds(z * LANES, LANES)
            ].astype(BF16)
    pieces(x_turned, held, outs, PIECES[:2])


def more_weights_kernel(x_turned, held, *outs):
    pieces(x_turned, held, outs, PIECES[2:])


def fold_kernel(own, low, low_more, high, high_more, *outs):
    for i, out in enumerate(outs):
        first, second = (low, low_more) if i < 2 else (high, high_more)
        out[...] = own[i] + first[i % 2] + second[i % 2]


def inputs_kernel(steps, grads, direct, weights, out):
    model = direct.shape[1]
    tokens, width = out.shape
    at = pl.ds(pl.multiple_of(pl.program_id(0) * width, width), width)
    total = direct[:, at]
    for half in range(2):
        total = total + dot(
            grads[half], weights[at, pl.ds(half * model, model)], ((1,), (1,))
        )
    unmove = jnp.where(order(tokens, steps, True), 1.0, 0.0).astype(BF16)
    out[...] = dot(unmove, total.astype(BF16)).astype(BF16)


def sum_kernel(scale, *refs):
    *parts, out = refs
    for z in range(out.shape[0]):
        at = pl.ds(z * LANES, LANES)
        total = parts[0][:, at]
        for value in parts[1:]:
            total = total + value[:, at]
        out[z] = total * scale


def params(mib):
    return pltpu.CompilerParams(vmem_limit_bytes=mib << 20)


def full(shape):
    return pl.BlockSpec(shape, lambda j: (0,) * len(shape))


def columns(rows, width=BLOCK, first=0):
    return pl.BlockSpec((rows, width), lambda j: (0, j + first))


def far(value):
    return pltpu.with_memory_space_constraint(value, pltpu.HBM)


def shaped(shape, dtype=F32):
    return jax.ShapeDtypeStruct(shape, dtype)


def gates(
    inputs, gate_in, cotangent, recon_mask, segment_starts, weights, gate_bias, decay_rate, peers
):
    rows, steps, model = inputs.shape
    tokens = rows * steps
    blocks = model // WIDTH
    flat = lambda value: value.reshape(tokens, model)
    bias = gate_bias.reshape(1, 2 * model)
    tile = columns(tokens, WIDTH)
    near = pl.BlockSpec(memory_space=pltpu.VMEM)
    return pl.pallas_call(
        gates_kernel,
        grid=(blocks,),
        in_specs=[
            full(segment_starts.shape),
            full((tokens, model)),
            tile,
            tile,
            full((rows, steps)),
            columns(model, WIDTH),
            columns(model, WIDTH, blocks),
            full((1, 2 * model)),
            full((1, model)),
        ],
        out_specs=[pl.BlockSpec((peers, 2 * rows, WIDTH), lambda j: (0, 0, j)), near, near, near],
        out_shape=[
            shaped((peers, 2 * rows, model)),
            pltpu.VMEM((3 * rows * GROUPS, model), F32),
            pltpu.VMEM((7, tokens, model), F32),
            pltpu.VMEM((tokens, model), F32),
        ],
        scratch_shapes=[
            pltpu.VMEM((tokens, tokens), BF16),
            pltpu.VMEM((tokens, tokens), BF16),
            pltpu.VMEM((tokens, model), BF16),
        ]
        + [pltpu.VMEM((tokens, WIDTH), F32)] * 4,
        compiler_params=params(PARAMS[0]),
        name="gates",
    )(
        far(segment_starts), far(flat(inputs)), far(flat(gate_in)), far(flat(cotangent)), far(recon_mask),
        far(weights), far(weights), far(bias), far(decay_rate.reshape(1, model)),
    )


def gradients(slabs, grouped, middle, xp):
    tokens, model = xp.shape
    near = pl.BlockSpec(memory_space=pltpu.VMEM)
    return pl.pallas_call(
        grads_kernel,
        grid=(model // SPAN,),
        in_specs=[near] * 4,
        out_specs=[columns(tokens, SPAN), near, near, near],
        out_shape=[
            shaped((tokens, model), BF16),
            pltpu.VMEM((2, tokens, model), BF16),
            pltpu.VMEM((2, tokens, model // 2), F32),
            pltpu.VMEM((tokens, model), F32),
        ],
        scratch_shapes=[pltpu.VMEM((tokens, SPAN), F32)] * 4,
        compiler_params=params(PARAMS[1]),
        name="grads",
    )(slabs, grouped, middle, xp)


def input_gradient(grads, direct, weights, steps):
    tokens, model = direct.shape
    near = pl.BlockSpec(memory_space=pltpu.VMEM)
    return pl.pallas_call(
        lambda *refs: inputs_kernel(steps, *refs),
        grid=(model // WIDE,),
        in_specs=[near] * 3,
        out_specs=columns(tokens, WIDE),
        out_shape=shaped((tokens, model), BF16),
        compiler_params=params(16),
        cost_estimate=pl.CostEstimate(
            flops=4 * tokens * model * model, bytes_accessed=6 * model * model, transcendentals=0
        ),
        name="inputs",
    )(grads, direct, weights)


def per_device(
    inputs, gate_in, cotangent, recon_mask, segment_starts, weights, gate_bias, decay_rate
):
    rows, steps, model = inputs.shape
    tokens = rows * steps
    peers, pairs = lax.axis_size("ctx"), lax.axis_size("dp")
    chips = pairs // 2
    summary, grouped, middle, xp = gates(
        inputs, gate_in, cotangent, recon_mask, segment_starts, weights, gate_bias, decay_rate, peers
    )
    slabs = lax.all_to_all(summary, "ctx", 0, 0, tiled=True)
    slabs, xp = lax.optimization_barrier((slabs, xp))
    swap = [(i, i ^ 1) for i in range(pairs)]
    x_other = lax.ppermute(xp, "dp", swap)
    part = model // peers
    gate_grad, grads, sent, direct = gradients(slabs, grouped, middle, xp)
    received = lax.ppermute(sent, "dp", swap)
    x_turned, held = pl.pallas_call(
        turn_kernel,
        out_shape=[shaped((model, 2 * tokens), BF16), shaped((2 * tokens, model), BF16)],
        compiler_params=params(8),
        name="turn",
    )(xp, x_other, grads)
    piece = shaped((2, part, model))
    held, on2, back2 = pl.pallas_call(
        first_weights_kernel,
        out_shape=[shaped((2 * tokens, model), BF16), piece, piece],
        compiler_params=params(12),
        input_output_aliases={2: 0},
        name="first_weights",
    )(x_turned, received, held)
    on1, back1, on_last, back_last, stay = pl.pallas_call(
        more_weights_kernel,
        out_shape=[piece] * 4 + [shaped((SIDE, part, model))],
        compiler_params=params(12),
        name="more_weights",
    )(x_turned, held)

    def move(value, step, first):
        pairs_of = []
        for i in range(peers * pairs):
            x, y, d = i // pairs // SIDE, i // pairs % SIDE, i % pairs
            if (d % 2 == 0) == first:
                x = (x + step) % SIDE
            else:
                y = (y + step) % SIDE
            pairs_of.append((i, (x * SIDE + y) * pairs + d))
        return lax.ppermute(value, ("ctx", "dp"), pairs_of)

    came_on2, came_back2 = move(on2, 1, True), move(back2, -1, True)
    came_on1, came_back1 = move(on1, 1, True), move(back1, -1, True)
    came_on1, came_back1, direct = lax.optimization_barrier((came_on1, came_back1, direct))
    came_on = move(on_last + came_on2, 1, True)
    came_back = move(back_last + came_back2, -1, True)
    input_grad = input_gradient(grads, direct, weights, steps)
    came_on, came_back, input_grad = lax.optimization_barrier((came_on, came_back, input_grad))
    scale = 1.0 / math.sqrt(rows * pairs * steps * peers)
    near = shaped((part, model))
    quarters = pl.pallas_call(
        fold_kernel,
        out_shape=[near] * SIDE,
        compiler_params=params(8),
        name="fold",
    )(stay, came_back1, came_on, came_on1, came_back)
    others = [move(quarters[d], d, False) for d in (2, 1, 3)]
    by_chip = pl.pallas_call(
        lambda *refs: sum_kernel(scale, *refs),
        out_shape=shaped((chips, part, LANES)),
        compiler_params=params(4),
        name="slab_sum",
    )(quarters[0], *others)
    same_core = [list(range(core, pairs, 2)) for core in range(2)]
    by_chip = lax.all_to_all(
        by_chip, "dp", 0, 0, axis_index_groups=same_core, tiled=True
    )
    total = jnp.sum(by_chip, axis=0)
    return (
        input_grad.reshape(inputs.shape),
        gate_grad.reshape(inputs.shape),
        total,
    )


def solution(mesh):
    return jax.shard_map(
        per_device,
        mesh=mesh,
        in_specs=(
            P("dp", "ctx", None),
            P("dp", "ctx", None),
            P("dp", "ctx", None),
            P("dp", "ctx"),
            P("dp", None),
            P(),
            P(),
            P(),
        ),
        out_specs=(P("dp", "ctx", None), P("dp", "ctx", None), P("ctx", "dp")),
        check_vma=False,
    )
```
